32 devices in a mesh: grp: 4 (over x, core), gx: 2 (over y), gy: 4 (over z).
Axes of the slice: x: 2, y: 2, z: 4, core: 2. Of those that a mesh axis runs over, the one named last changes fastest.
Arguments:
- slot_field: float32 [4, 2, 96, 512], P('grp', None, 'gx', 'gy'), may hold values from -6 to 6
- solid: int32 [2, 96, 512], P(None, 'gx', 'gy'), may hold values 0 or 1
- lift_weight: bfloat16 [3, 64], replicated, may hold values from -3.5 to 3.5
- spectral_weight: bfloat16 [2048, 128], replicated, may hold values from -1.5 to 1.5
- mix_weight: bfloat16 [64, 64], replicated, may hold values from -0.75 to 0.75
- project_weight: bfloat16 [64, 3], replicated, may hold values from -0.75 to 0.75
- mode_index: int32 [32], replicated, may hold values from 0 to 47, as said below
Outputs:
- new_velocity: float32 [3, 2, 96, 512], P(None, None, 'gx', 'gy')
- spectral_grad: float32 [2048, 128], P(('grp', 'gx', 'gy'))
- mix_grad: float32 [64, 64], replicated
The draws below stay inside these ranges and needn't reach their ends.
Inputs may be any that keep to these rules, and one draw needn't show every extreme that they name: `mode_index`: 32 distinct values in ascending order; 0 and 47 are always among them.
All inputs are finite; a program needn't handle non-finite values. No bound on the sum of `solid` on one device may be relied on, other than what follows from the above.
Results may differ from the reference program's by a relative error of at most 0.0013.
Values may be sent and summed in bfloat16 or wider, within the bound.
A program may use at most 64 MiB of HBM per device.

```python
import math
import jax
import jax.numpy as jnp
from jax import lax

WIDTH = 64
MODES = 32
MODE_RANGE = 48
NX = 96
NY = 512
NZ = 2
N_GRP = 4


def draw_mode_index(key, part):
    key = jax.random.fold_in(key, 7)
    inner = (jax.random.permutation(key, MODE_RANGE - 2) + 1).astype(jnp.int32)
    chosen = jnp.concatenate([jnp.zeros((1,), jnp.int32), inner[:MODES - 2], jnp.full((1,), MODE_RANGE - 1, jnp.int32)])
    return jnp.sort(chosen)


def set_ends(array, key, least, top_value):
    place = [jax.random.randint(jax.random.fold_in(key, axis), (), 0, length) for axis, length in enumerate(array.shape)]
    main_axis = array.shape.index(max(array.shape))
    next_to = place[:main_axis] + [(place[main_axis] + 1) % array.shape[main_axis]] + place[main_axis + 1:]
    return array.at[tuple(place)].set(least).at[tuple(next_to)].set(top_value)


def shard_levels(stream_key, extent, shards, low, high):
    loudness, own = 1.0, jax.random.fold_in(stream_key, 6)
    for dim, shards_of in shards:
        steps = jnp.exp(jax.random.uniform(jax.random.fold_in(own, dim), (shards_of,), jnp.float32, low / len(shards), high / len(shards)))
        loudness = loudness * jnp.repeat(steps, extent[dim] // shards_of).reshape([-1 if axis == dim else 1 for axis in range(len(extent))])
    return loudness


def centred(stream_key, extent, spread, most, shards=(), kind=jnp.bfloat16):
    factor_of = shard_levels(stream_key, extent, shards, -0.22, 0.18) if shards else 1.0
    drawn = jax.random.normal(stream_key, extent, jnp.float32) * spread * factor_of
    return jnp.minimum(jnp.maximum(drawn, -most), most).astype(kind)


def setup_inputs(seed: int = 0) -> dict:
    key_list = jax.random.split(jax.random.key(seed), 8)
    slot_field = centred(key_list[0], (N_GRP, NZ, NX, NY), 1.0, 6.0, ((0, 4), (2, 2), (3, 4)), jnp.float32)
    solid = set_ends((jax.random.randint(key_list[1], (NZ, NX, NY), 0, 8) < 1).astype(jnp.int32), jax.random.fold_in(key_list[1], 1), 0, 1)
    lift_weight = centred(key_list[2], (3, WIDTH), 3 ** -0.5, 3.5)
    spectral_weight = centred(key_list[3], (MODES * WIDTH, 2 * WIDTH), 0.25, 1.5)
    mix_weight = centred(key_list[4], (WIDTH, WIDTH), WIDTH ** -0.5, 0.75)
    project_weight = centred(key_list[5], (WIDTH, 3), WIDTH ** -0.5, 0.75)
    mode_index = draw_mode_index(jax.random.fold_in(key_list[7], 71), 0)
    return {"slot_field": slot_field, "solid": solid, "lift_weight": lift_weight, "spectral_weight": spectral_weight, "mix_weight": mix_weight, "project_weight": project_weight, "mode_index": mode_index}


VISCOSITY = 0.05
TIME_STEP = 0.1

def interior(source):
    return source[1:-1, 1:-1, 1:-1]

def along_x(source):
    return 0.5 * (source[1:-1, 2:, 1:-1] - source[1:-1, :-2, 1:-1])

def along_y(source):
    return 0.5 * (source[1:-1, 1:-1, 2:] - source[1:-1, 1:-1, :-2])

def along_z(source):
    return 0.5 * (source[2:, 1:-1, 1:-1] - source[:-2, 1:-1, 1:-1])

def laplace(source):
    total = source[2:, 1:-1, 1:-1] + source[:-2, 1:-1, 1:-1]
    total = total + source[1:-1, 2:, 1:-1] + source[1:-1, :-2, 1:-1]
    total = total + source[1:-1, 1:-1, 2:] + source[1:-1, 1:-1, :-2]
    return total - 6.0 * interior(source)

def section_component(padded, component, solid):
    source = padded[component]
    velocity = [interior(padded[index]) for index in range(3)]
    advect = velocity[0] * along_x(source) + velocity[1] * along_y(source) + velocity[2] * along_z(source)
    pressure = padded[3]
    press_grad = jnp.stack([along_x(pressure), along_y(pressure), along_z(pressure)])[component]
    update = interior(source) + TIME_STEP * (VISCOSITY * laplace(source) - advect - press_grad)
    return update * (1.0 - solid.astype(jnp.float32))

def spectral_table(mode_index, x_length):
    places = jnp.arange(x_length, dtype=jnp.int32)
    phases = mode_index[:, None] * places[None, :] % x_length
    angles = 2.0 * jnp.pi / x_length * phases.astype(jnp.float32)
    return jnp.concatenate([jnp.cos(angles), -jnp.sin(angles)], axis=0).astype(jnp.bfloat16)

def contract(form, left, right):
    return jnp.einsum(form, left.astype(jnp.float32), right.astype(jnp.float32))

def student_terms(line_data, dft_table, lift_weight, spectral_weight, mix_weight, project_weight, loss_scale, x_length):
    mode_count = dft_table.shape[0] // 2
    chan_count = mix_weight.shape[0]
    scale_dft = 1.0 / math.sqrt(x_length)
    old_part = line_data[:3]
    target = line_data[3:].astype(jnp.float32)
    lifted = contract('iln,ic->cln', old_part, lift_weight).astype(jnp.bfloat16)
    coeffs = (contract('cln,mn->clm', lifted, dft_table) * scale_dft).astype(jnp.bfloat16)
    real_in = coeffs[..., :mode_count]
    imag_in = coeffs[..., mode_count:]
    weights = spectral_weight.reshape(mode_count, chan_count, 2 * chan_count)
    real_w = weights[..., :chan_count]
    imag_w = weights[..., chan_count:]
    real_out = contract('clm,mco->olm', real_in, real_w) - contract('clm,mco->olm', imag_in, imag_w)
    imag_out = contract('clm,mco->olm', real_in, imag_w) + contract('clm,mco->olm', imag_in, real_w)
    mixed = jnp.concatenate([real_out, imag_out], axis=2).astype(jnp.bfloat16)
    spectral = contract('olm,mn->oln', mixed, dft_table) * (2.0 * scale_dft)
    local_term = contract('cln,co->oln', lifted, mix_weight)
    hidden = spectral + local_term
    active, gelu_back = jax.vjp(jax.nn.gelu, hidden)
    active = active.astype(jnp.bfloat16)
    predicted = contract('oln,oi->iln', active, project_weight)
    misfit = (predicted - target) * loss_scale
    back_active = jnp.einsum('iln,oi->oln', misfit, project_weight.astype(jnp.float32), precision=lax.Precision.HIGHEST)
    back_hidden = gelu_back(back_active)[0].astype(jnp.bfloat16)
    mix_part = contract('cln,oln->co', lifted, back_hidden)
    back_mixed = (contract('oln,mn->olm', back_hidden, dft_table) * (2.0 * scale_dft)).astype(jnp.bfloat16)
    back_real = back_mixed[..., :mode_count]
    back_imag = back_mixed[..., mode_count:]
    grad_real = contract('clm,olm->mco', real_in, back_real) + contract('clm,olm->mco', imag_in, back_imag)
    grad_imag = contract('clm,olm->mco', real_in, back_imag) - contract('clm,olm->mco', imag_in, back_real)
    spectral_part = jnp.concatenate([grad_real, grad_imag], axis=2).reshape(mode_count * chan_count, 2 * chan_count)
    return (spectral_part, mix_part)

def reference(slot_field, solid, lift_weight, spectral_weight, mix_weight, project_weight, mode_index):
    padded = jnp.pad(slot_field, ((0, 0), (1, 1), (1, 1), (1, 1)))
    new_velocity = jnp.stack([section_component(padded, component, solid) for component in range(3)])
    fields = jnp.concatenate([slot_field[:3], new_velocity], axis=0).astype(jnp.bfloat16)
    line_count = NZ * NY
    line_data = jnp.transpose(fields, (0, 1, 3, 2)).reshape(6, line_count, NX)
    block_rows = math.gcd(line_count, 128)
    blocks = jnp.transpose(line_data.reshape(6, line_count // block_rows, block_rows, NX), (1, 0, 2, 3))
    dft_table = spectral_table(mode_index, NX)
    loss_scale = 16.0 / math.sqrt(NX * NY * NZ)

    def scan_step(totals, line_block):
        spec_part, mix_part = student_terms(line_block, dft_table, lift_weight, spectral_weight, mix_weight, project_weight, loss_scale, NX)
        return ((totals[0] + spec_part, totals[1] + mix_part), None)
    starting = (jnp.zeros(spectral_weight.shape, jnp.float32), jnp.zeros(mix_weight.shape, jnp.float32))
    (spec_total, mix_total), _ = lax.scan(scan_step, starting, blocks)
    return (new_velocity, spec_total, mix_total)
```

```python
import functools
import math

import jax
import jax.numpy as jnp
from jax import lax
from jax.experimental import pallas as pl
from jax.experimental.pallas import tpu as pltpu
from jax.sharding import PartitionSpec as P

VISCOSITY = 0.05
TIME_STEP = 0.1


def with_halo(block, sides, width):
    for axis, dim in sides:
        count = lax.axis_size(axis)
        forward = [(i, i + 1) for i in range(count - 1)]
        backward = [(target, source) for source, target in forward]
        low = lax.ppermute(
            lax.slice_in_dim(block, block.shape[dim] - width, None, axis=dim), axis, forward
        )
        high = lax.ppermute(lax.slice_in_dim(block, 0, width, axis=dim), axis, backward)
        block = jnp.concatenate([low, block, high], axis=dim)
    return block


def interior(source):
    return source[1:-1, 1:-1, 1:-1]


def along_x(source):
    return 0.5 * (source[1:-1, 2:, 1:-1] - source[1:-1, :-2, 1:-1])


def along_y(source):
    return 0.5 * (source[1:-1, 1:-1, 2:] - source[1:-1, 1:-1, :-2])


def along_z(source):
    return 0.5 * (source[2:, 1:-1, 1:-1] - source[:-2, 1:-1, 1:-1])


def laplace(source):
    total = source[2:, 1:-1, 1:-1] + source[:-2, 1:-1, 1:-1]
    total = total + source[1:-1, 2:, 1:-1] + source[1:-1, :-2, 1:-1]
    total = total + source[1:-1, 1:-1, 2:] + source[1:-1, 1:-1, :-2]
    return total - 6.0 * interior(source)


def section_component(padded, component, solid):
    source = padded[component]
    velocity = [interior(padded[index]) for index in range(3)]
    advect = (
        velocity[0] * along_x(source)
        + velocity[1] * along_y(source)
        + velocity[2] * along_z(source)
    )
    pressure = padded[3]
    press_grad = jnp.stack([along_x(pressure), along_y(pressure), along_z(pressure)])[component]
    update = interior(source) + TIME_STEP * (VISCOSITY * laplace(source) - advect - press_grad)
    return update * (1.0 - solid.astype(jnp.float32))


def spectral_table(mode_index, x_length):
    places = jnp.arange(x_length, dtype=jnp.int32)
    phases = mode_index[:, None] * places[None, :] % x_length
    angles = 2.0 * jnp.pi / x_length * phases.astype(jnp.float32)
    return jnp.concatenate([jnp.cos(angles), -jnp.sin(angles)], axis=0).astype(jnp.bfloat16)


def contract(form, left, right):
    return jnp.einsum(form, left, right, preferred_element_type=jnp.float32)


def student_terms(
    line_data,
    dft_table,
    lift_weight,
    spectral_weight,
    mix_weight,
    project_weight,
    loss_scale,
    x_length,
):
    mode_count = dft_table.shape[0] // 2
    chan_count = mix_weight.shape[0]
    scale_dft = 1.0 / math.sqrt(x_length)
    old_part = line_data[:3]
    target = line_data[3:].astype(jnp.float32)
    lifted = contract("iln,ic->cln", old_part, lift_weight).astype(jnp.bfloat16)
    coeffs = (contract("cln,mn->clm", lifted, dft_table) * scale_dft).astype(jnp.bfloat16)
    real_in = coeffs[..., :mode_count]
    imag_in = coeffs[..., mode_count:]
    weights = spectral_weight.reshape(mode_count, chan_count, 2 * chan_count)
    real_w = weights[..., :chan_count]
    imag_w = weights[..., chan_count:]
    real_out = contract("clm,mco->olm", real_in, real_w) - contract("clm,mco->olm", imag_in, imag_w)
    imag_out = contract("clm,mco->olm", real_in, imag_w) + contract("clm,mco->olm", imag_in, real_w)
    mixed = jnp.concatenate([real_out, imag_out], axis=2).astype(jnp.bfloat16)
    spectral = contract("olm,mn->oln", mixed, dft_table) * (2.0 * scale_dft)
    local_term = contract("cln,co->oln", lifted, mix_weight)
    hidden = spectral + local_term
    active, gelu_back = jax.vjp(jax.nn.gelu, hidden)
    active = active.astype(jnp.bfloat16)
    predicted = contract("oln,oi->iln", active, project_weight)
    misfit = (predicted - target) * loss_scale
    back_active = jnp.einsum(
        "iln,oi->oln", misfit, project_weight.astype(jnp.float32), precision=lax.Precision.HIGHEST
    )
    back_hidden = gelu_back(back_active)[0].astype(jnp.bfloat16)
    mix_part = contract("cln,oln->co", lifted, back_hidden)
    back_mixed = (contract("oln,mn->olm", back_hidden, dft_table) * (2.0 * scale_dft)).astype(
        jnp.bfloat16
    )
    back_real = back_mixed[..., :mode_count]
    back_imag = back_mixed[..., mode_count:]
    grad_real = contract("clm,olm->mco", real_in, back_real) + contract(
        "clm,olm->mco", imag_in, back_imag
    )
    grad_imag = contract("clm,olm->mco", real_in, back_imag) - contract(
        "clm,olm->mco", imag_in, back_real
    )
    spectral_part = jnp.concatenate([grad_real, grad_imag], axis=2).reshape(
        mode_count * chan_count, 2 * chan_count
    )
    return (spectral_part, mix_part)


def general(slot_field, solid, lift_weight, spectral_weight, mix_weight, project_weight, mode_index):
    role_index = lax.axis_index("grp")
    own_tile = slot_field[0]
    planes, x_rows, y_cols = own_tile.shape
    x_length = x_rows * lax.axis_size("gx")
    cell_total = x_length * y_cols * lax.axis_size("gy") * planes
    loss_scale = 16.0 / math.sqrt(cell_total)
    dft_table = spectral_table(mode_index, x_length)
    rimmed = with_halo(own_tile, (("gx", 1), ("gy", 2)), 1)
    gathered = lax.all_gather(rimmed[None], "grp", axis=0, tiled=True)
    padded = jnp.pad(gathered, ((0, 0), (1, 1), (0, 0), (0, 0)))
    old_velocity = gathered[:3, :, 1:-1, 1:-1]
    new_tile = lax.cond(
        role_index < 3,
        lambda: section_component(padded, jnp.minimum(role_index, 2), solid),
        lambda: own_tile,
    )
    new_slots = lax.all_gather(new_tile[None], "grp", axis=0, tiled=True)
    new_velocity = new_slots[:3]
    both_fields = jnp.concatenate([old_velocity, new_velocity], axis=0).astype(jnp.bfloat16)
    pencil_data = lax.all_to_all(
        jnp.transpose(both_fields, (0, 1, 3, 2)), "gx", split_axis=2, concat_axis=3, tiled=True
    )
    line_data = pencil_data.reshape(6, -1, x_length)

    def student(own_lines):
        return student_terms(
            own_lines,
            dft_table,
            lift_weight,
            spectral_weight,
            mix_weight,
            project_weight,
            loss_scale,
            x_length,
        )

    def nothing():
        return (
            jnp.zeros(spectral_weight.shape, jnp.float32),
            jnp.zeros(mix_weight.shape, jnp.float32),
        )

    spectral_part, mix_part = lax.cond(role_index == 3, lambda: student(line_data), nothing)
    spectral_grad = lax.psum_scatter(
        spectral_part, ("grp", "gx", "gy"), scatter_dimension=0, tiled=True
    )
    mix_grad = lax.psum(mix_part, ("grp", "gx", "gy"))
    return (new_velocity, spectral_grad, mix_grad)


MESH = pl.DeviceIdType.MESH
BF = jnp.bfloat16
F32 = jnp.float32


def dot(left, right, contract_dims=((1,), (0,))):
    return lax.dot_general(left, right, (contract_dims, ((), ())), preferred_element_type=F32)


def iota(shape, dim):
    return lax.broadcasted_iota(jnp.int32, shape, dim)


def fused_kernel(
    sizes,
    field_ref,
    solid_ref,
    lift_ref,
    spec_ref,
    mix_ref,
    proj_ref,
    mode_ref,
    newv_ref,
    grad_ref,
    mixg_ref,
    gath,
    both_solid,
    edge,
    rims,
    fresh,
    wide_mix,
    lift_big,
    proj_down,
    proj_up,
    lifted_ref,
    slope_ref,
    stage,
    stage_out,
    a_own,
    d_own,
    a_all,
    d_all,
    m_part,
    m_recv,
    m_row,
    field_send,
    field_recv,
    solid_sem,
    rim_send,
    rim_recv,
    a_send,
    a_recv,
    d_send,
    d_recv,
    m_send,
    m_sem,
    r_send,
    r_recv,
):
    grps, gxs, gys, x_length, cell_total = sizes
    count = grps * gxs * gys
    near = grps * gxs
    half = x_length // gxs
    modes = count
    lines = 32
    pairs = lines // 2
    chans = 64
    g = lax.axis_index("grp")
    gx = lax.axis_index("gx")
    gy = lax.axis_index("gy")
    me = (g * gxs + gx) * gys + gy
    slot = g * gxs + gx
    scale_dft = 1.0 / math.sqrt(x_length)
    loss_scale = 16.0 / math.sqrt(cell_total)

    def flat_id(t):
        return {"grp": t // (gxs * gys), "gx": (t // gys) % gxs, "gy": t % gys}

    def near_id(s, z):
        return {"grp": s // gxs, "gx": s % gxs, "gy": z}

    def others(body, total=count, mine=me):
        def step(k, carry):
            body((mine + k) % total)
            return carry

        lax.fori_loop(1, total, step, 0)

    barrier = pltpu.get_barrier_semaphore()
    others(lambda t: pl.semaphore_signal(barrier, inc=1, device_id=flat_id(t), device_id_type=MESH))

    own = field_ref[0]
    flat = jnp.concatenate([own.reshape(2 * half, 128), jnp.zeros((128 - 2 * half, 128), F32)], axis=0)
    turned = jnp.transpose(flat)
    edge[0] = turned[0:1, :]
    edge[1] = turned[127:128, :]
    gath[pl.ds(slot, 1)] = own[None]
    both_solid[pl.ds(gx, 1)] = solid_ref[...][None]

    @pl.when(gy == 0)
    def _():
        rims[0] = jnp.zeros((near, 1, 128), F32)

    @pl.when(gy == gys - 1)
    def _():
        rims[1] = jnp.zeros((near, 1, 128), F32)

    pl.semaphore_wait(barrier, count - 1)

    def field_copy(s):
        return pltpu.make_async_remote_copy(
            src_ref=field_ref.at[0],
            dst_ref=gath.at[slot],
            send_sem=field_send.at[s],
            recv_sem=field_recv.at[slot],
            device_id=near_id(s, gy),
            device_id_type=MESH,
        )

    def field_arrival(s):
        return pltpu.make_async_remote_copy(
            src_ref=field_ref.at[0],
            dst_ref=gath.at[s],
            send_sem=field_send.at[s],
            recv_sem=field_recv.at[s],
            device_id=near_id(s, gy),
            device_id_type=MESH,
        )

    def rim_copy(side, s):
        return pltpu.make_async_remote_copy(
            src_ref=edge.at[side],
            dst_ref=rims.at[1 - side, slot],
            send_sem=rim_send.at[side, s],
            recv_sem=rim_recv.at[1 - side, slot],
            device_id=near_id(s, gy - 1 + 2 * side),
            device_id_type=MESH,
        )

    def rim_arrival(side, s):
        return pltpu.make_async_remote_copy(
            src_ref=edge.at[1 - side],
            dst_ref=rims.at[side, s],
            send_sem=rim_send.at[1 - side, s],
            recv_sem=rim_recv.at[side, s],
            device_id=near_id(s, gy - 1 + 2 * side),
            device_id_type=MESH,
        )

    def solid_copy(place):
        return pltpu.make_async_remote_copy(
            src_ref=solid_ref,
            dst_ref=both_solid.at[place],
            send_sem=solid_sem.at[0],
            recv_sem=solid_sem.at[1],
            device_id={"grp": g, "gx": 1 - gx, "gy": gy},
            device_id_type=MESH,
        )

    def each_near(body):
        def step(s, carry):
            body(s)
            return carry

        lax.fori_loop(0, near, step, 0)

    others(lambda s: field_copy(s).start(), near, slot)
    solid_copy(gx).start()

    @pl.when(gy > 0)
    def _():
        each_near(lambda s: rim_copy(0, s).start())

    @pl.when(gy < gys - 1)
    def _():
        each_near(lambda s: rim_copy(1, s).start())

    lane = iota((x_length, 128), 1)
    low64 = iota((16, 128), 1) < 64
    mode_row = mode_ref[...].astype(F32)
    mode_row = jnp.concatenate([mode_row] * 4, axis=1)
    place = iota((x_length, 128), 0).astype(F32)
    raw = mode_row * place + jnp.where(lane >= modes, 0.25 * x_length, 0.0)
    phase = raw - x_length * jnp.floor((raw + 0.5) * (1.0 / x_length))
    phase = jnp.where(phase >= 0.5 * x_length, phase - x_length, phase)
    angle = phase * (math.pi / x_length)
    square = angle * angle
    series = jnp.full_like(square, -1.0 / 39916800.0)
    for term in (1.0 / 362880.0, -1.0 / 5040.0, 1.0 / 120.0, -1.0 / 6.0, 1.0):
        series = series * square + term
    sine = series * angle
    waves = 1.0 - 2.0 * sine * sine
    table_t = waves[:, : 2 * modes].astype(BF)
    table = jnp.transpose(jnp.concatenate([waves, jnp.zeros((128 - x_length, 128), F32)], axis=0))
    table = table[: 2 * modes, :x_length].astype(BF)

    row128 = iota((128, 128), 0)
    col128 = iota((128, 128), 1)
    lift = lift_ref[...].astype(F32)
    lift = jnp.concatenate([lift, lift], axis=1)
    lift_rows = jnp.where(
        row128 < 32,
        lift[0:1],
        jnp.where(row128 < 64, lift[1:2], jnp.where(row128 < 96, lift[2:3], 0.0)),
    )
    proj = proj_ref[...].astype(F32)
    col64 = iota((64, 128), 1)
    proj_cols = jnp.where(
        col64 < 32,
        proj[:, 0:1],
        jnp.where(col64 < 64, proj[:, 1:2], jnp.where(col64 < 96, proj[:, 2:3], 0.0)),
    )
    proj_rows = jnp.transpose(proj_cols)
    proj_rows = jnp.concatenate([proj_rows, proj_rows], axis=1)
    line_of_row = jnp.bitwise_and(row128, 31)
    half_of_lane = jnp.where(col128 < 64, 0, 1)
    line_of_col = jnp.bitwise_and(col64, 31)

    def widen(p, carry):
        hit = line_of_row == 2 * p + half_of_lane
        cols = pl.ds(pl.multiple_of(p * 128, 128), 128)
        lift_big[:, cols] = jnp.where(hit, lift_rows, 0.0).astype(BF)
        up = jnp.where(hit, proj_rows, 0.0).astype(BF)
        proj_up[0:128, cols] = up
        proj_up[128:256, cols] = up
        for part in range(2):
            down = jnp.where(line_of_col == 2 * p + part, proj_cols, 0.0).astype(BF)
            proj_down[pl.ds(pl.multiple_of(p * 128 + part * 64, 64), 64), :] = down
        return carry

    lax.fori_loop(0, pairs, widen, 0)

    low_half = col64 < 64

    def widen_mix(m, carry):
        block = spec_ref[pl.ds(pl.multiple_of(m * 64, 64), 64), :]
        wide = block.astype(F32)
        turned_block = pltpu.roll(wide, 64, 1)
        wide_mix[m, 0:64, :] = block
        wide_mix[m, 64:128, :] = jnp.where(low_half, -turned_block, turned_block).astype(BF)
        return carry

    lax.fori_loop(0, modes, widen_mix, 0)

    mix = mix_ref[...].astype(F32)
    mix = jnp.concatenate([mix, mix], axis=1)
    mix = jnp.concatenate([mix, mix], axis=0)
    mix = jnp.where((row128 < 64) == (col128 < 64), mix, 0.0)
    blank = jnp.zeros_like(mix)
    mix_four = jnp.concatenate(
        [jnp.concatenate([mix, blank], axis=1), jnp.concatenate([blank, mix], axis=1)], axis=0
    ).astype(BF)
    pick = jnp.concatenate(
        [
            jnp.where((col128 // 32 == i) & (row128 == 32 * g + jnp.bitwise_and(col128, 31)), 1.0, 0.0)
            for i in range(3)
        ],
        axis=0,
    ).astype(BF)

    others(lambda s: field_arrival(s).wait_recv(), near, slot)
    solid_copy(1 - gx).wait_recv()

    @pl.when(gy > 0)
    def _():
        each_near(lambda s: rim_arrival(0, s).wait_recv())

    @pl.when(gy < gys - 1)
    def _():
        each_near(lambda s: rim_arrival(1, s).wait_recv())

    rim_rows = [rims[side, s] for side in range(2) for s in range(near)]
    rim_rows.append(jnp.zeros((128 - 2 * near, 128), F32))
    rim_cols = jnp.transpose(jnp.concatenate(rim_rows, axis=0))
    first_row = iota((x_length, 128), 0) == 0
    last_row = iota((x_length, 128), 0) == x_length - 1

    def whole(f, z):
        return jnp.concatenate([gath[f * gxs + h, z] for h in range(gxs)], axis=0)

    def rim(f, z, side):
        cols = [
            rim_cols[z * half : (z + 1) * half, side * near + f * gxs + h :][:, 0:1] for h in range(gxs)
        ]
        return jnp.concatenate(cols, axis=0)

    def shifted(f, z, value):
        x_up = jnp.where(last_row, 0.0, pltpu.roll(value, x_length - 1, 0))
        x_down = jnp.where(first_row, 0.0, pltpu.roll(value, 1, 0))
        y_up = jnp.where(lane == 127, rim(f, z, 1), pltpu.roll(value, 127, 1))
        y_down = jnp.where(lane == 0, rim(f, z, 0), pltpu.roll(value, 1, 1))
        return x_up, x_down, y_up, y_down

    for z in range(2):
        fluid = 1.0 - jnp.concatenate([both_solid[h, z] for h in range(gxs)], axis=0).astype(F32)
        here = [whole(f, z) for f in range(4)]
        there = [whole(f, 1 - z) for f in range(4)]
        sign_z = 0.5 if z == 0 else -0.5
        press = shifted(3, z, here[3])
        grads = (0.5 * (press[0] - press[1]), 0.5 * (press[2] - press[3]), sign_z * there[3])
        for k in range(3):
            x_up, x_down, y_up, y_down = shifted(k, z, here[k])
            lap = there[k] + x_up + x_down + y_up + y_down - 6.0 * here[k]
            advect = (
                here[0] * (0.5 * (x_up - x_down))
                + here[1] * (0.5 * (y_up - y_down))
                + here[2] * (sign_z * there[k])
            )
            update = here[k] + TIME_STEP * (VISCOSITY * lap - advect - grads[k])
            update = update * fluid
            for h in range(gxs):
                fresh[k, z, h] = update[h * half : (h + 1) * half]
    for k in range(3):
        for z in range(2):
            newv_ref[k, z] = fresh[k, z, gx]

    old = [jnp.concatenate([gath[i * gxs + h, gx] for h in range(gxs)], axis=0) for i in range(3)]
    new = [jnp.concatenate([fresh[i, gx, h] for h in range(gxs)], axis=0) for i in range(3)]
    stacked = jnp.concatenate([jnp.concatenate(old, axis=1), jnp.concatenate(new, axis=1)], axis=0)
    picked = dot(stacked.astype(BF), pick)
    source = picked[:x_length].astype(BF)
    target = picked[x_length:]

    for b in range(pairs // 2):
        cols = slice(b * 256, (b + 1) * 256)
        lifted = dot(source, lift_big[:, cols]).astype(BF)
        lifted_ref[:, cols] = lifted
        coeffs = dot(table, lifted) * scale_dft
        stage[2 * b * 64 : (2 * b + 1) * 64, :] = coeffs[:, :128]
        stage[(2 * b + 1) * 64 : (2 * b + 2) * 64, :] = coeffs[:, 128:]

    def gather_mode(into):
        def step(m, carry):
            real = stage[pl.ds(m, pairs, stride=64), :]
            imag = stage[pl.ds(modes + m, pairs, stride=64), :]
            top = jnp.where(low64, real, pltpu.roll(imag, 64, 1))
            bottom = jnp.where(low64, pltpu.roll(real, 64, 1), imag)
            into[m] = jnp.concatenate([top, bottom], axis=0).astype(BF)
            return carry

        lax.fori_loop(0, modes, step, 0, unroll=4)

    def exchange(own_ref, all_ref, send, recv, t, slot_at):
        return pltpu.make_async_remote_copy(
            src_ref=own_ref.at[t],
            dst_ref=all_ref.at[slot_at],
            send_sem=send.at[t],
            recv_sem=recv.at[slot_at],
            device_id=flat_id(t),
            device_id_type=MESH,
        )

    gather_mode(a_own)
    others(lambda t: exchange(a_own, a_all, a_send, a_recv, t, me).start())
    a_all[pl.ds(me, 1)] = a_own[pl.ds(me, 1)]

    def mix_mode(m, carry):
        out = dot(a_own[m], wide_mix[m])
        top, bottom = out[:pairs], out[pairs:]
        stage_out[pl.ds(m, pairs, stride=64), :] = jnp.where(low64, top, pltpu.roll(bottom, 64, 1))
        stage_out[pl.ds(modes + m, pairs, stride=64), :] = jnp.where(
            low64, pltpu.roll(top, 64, 1), bottom
        )
        return carry

    lax.fori_loop(0, modes, mix_mode, 0, unroll=4)

    root = math.sqrt(2.0 / math.pi)
    predicted = jnp.zeros((x_length, 128), F32)
    for b in range(pairs // 2):
        cols = slice(b * 256, (b + 1) * 256)
        mixed = jnp.concatenate(
            [
                stage_out[2 * b * 64 : (2 * b + 1) * 64, :],
                stage_out[(2 * b + 1) * 64 : (2 * b + 2) * 64, :],
            ],
            axis=1,
        ).astype(BF)
        hidden = dot(table_t, mixed) * (2.0 * scale_dft) + dot(lifted_ref[:, cols], mix_four)
        squared = hidden * hidden
        bent = jnp.tanh(root * hidden * (1.0 + 0.044715 * squared))
        upper = 0.5 * (1.0 + bent)
        active = (hidden * upper).astype(BF)
        slope_ref[:, cols] = upper + 0.5 * hidden * (1.0 - bent * bent) * (
            root * (1.0 + 3.0 * 0.044715 * squared)
        )
        predicted = predicted + dot(active, proj_down[b * 256 : (b + 1) * 256, :])
    misfit = (predicted - target) * loss_scale
    coarse = misfit.astype(BF)
    fine = (misfit - coarse.astype(F32)).astype(BF)
    misfit_parts = jnp.concatenate([coarse, fine], axis=1)

    mix_sum = jnp.zeros((128, 128), F32)
    for b in range(pairs // 2):
        cols = slice(b * 256, (b + 1) * 256)
        back_active = dot(misfit_parts, proj_up[:, cols])
        back_hidden = (slope_ref[:, cols] * back_active).astype(BF)
        lifted = lifted_ref[:, cols]
        for part in range(2):
            lanes = slice(part * 128, (part + 1) * 128)
            mix_sum = mix_sum + dot(lifted[:, lanes], back_hidden[:, lanes], ((0,), (0,)))
        back = dot(table, back_hidden) * (2.0 * scale_dft)
        stage[2 * b * 64 : (2 * b + 1) * 64, :] = back[:, :128]
        stage[(2 * b + 1) * 64 : (2 * b + 2) * 64, :] = back[:, 128:]

    mix_own = mix_sum[:64] + pltpu.roll(mix_sum[64:], 64, 1)
    packed = jnp.where(iota((32, 128), 1) < 64, mix_own[:32], pltpu.roll(mix_own[32:], 64, 1))
    for row in range(count):
        m_part[row] = packed[row : row + 1, :]
    others(lambda t: exchange(m_part, m_recv, m_send, m_sem, t, me).start())
    m_recv[pl.ds(me, 1)] = m_part[pl.ds(me, 1)]

    gather_mode(d_own)
    others(lambda t: exchange(d_own, d_all, d_send, d_recv, t, me).start())
    d_all[pl.ds(me, 1)] = d_own[pl.ds(me, 1)]

    def row_copy(t, slot_at):
        return pltpu.make_async_remote_copy(
            src_ref=m_row,
            dst_ref=mixg_ref.at[slot_at],
            send_sem=r_send.at[t],
            recv_sem=r_recv.at[slot_at],
            device_id=flat_id(t),
            device_id_type=MESH,
        )

    others(lambda t: exchange(m_part, m_recv, m_send, m_sem, t, t).wait_recv())
    total = jnp.sum(m_recv[...], axis=0)
    m_row[...] = total
    mixg_ref[pl.ds(me, 1)] = total[None]
    others(lambda t: row_copy(t, me).start())

    others(lambda t: exchange(a_own, a_all, a_send, a_recv, t, t).wait_recv())
    others(lambda t: exchange(d_own, d_all, d_send, d_recv, t, t).wait_recv())
    a_lines = a_all[...].reshape(count * lines, 2 * chans)
    d_lines = d_all[...].reshape(count * lines, 2 * chans)
    square_sum = dot(a_lines, d_lines, ((0,), (0,)))
    turned_sum = pltpu.roll(square_sum[64:], 64, 1)
    grad_ref[...] = square_sum[:64] + jnp.where(low_half, turned_sum, -turned_sum)

    others(lambda t: row_copy(t, t).wait_recv())
    others(lambda s: field_copy(s).wait_send(), near, slot)
    solid_copy(gx).wait_send()

    @pl.when(gy > 0)
    def _():
        each_near(lambda s: rim_copy(0, s).wait_send())

    @pl.when(gy < gys - 1)
    def _():
        each_near(lambda s: rim_copy(1, s).wait_send())

    def finish(t):
        exchange(a_own, a_all, a_send, a_recv, t, me).wait_send()
        exchange(d_own, d_all, d_send, d_recv, t, me).wait_send()
        exchange(m_part, m_recv, m_send, m_sem, t, me).wait_send()
        row_copy(t, me).wait_send()

    others(finish)


def fused(sizes, slot_field, solid, lift_weight, spectral_weight, mix_weight, project_weight, mode_index):
    grps, gxs, gys, x_length, _ = sizes
    count = grps * gxs * gys
    near = grps * gxs
    half = x_length // gxs
    dma = pltpu.SemaphoreType.DMA
    vmem = pl.BlockSpec(memory_space=pltpu.VMEM)
    shape = jax.ShapeDtypeStruct
    new_velocity, spectral_grad, mix_rows = pl.pallas_call(
        functools.partial(fused_kernel, sizes),
        out_shape=(
            shape((3, 2, half, 128), F32),
            shape((64, 128), F32),
            shape((count, 1, 128), F32),
        ),
        in_specs=[vmem] * 7,
        out_specs=(vmem, vmem, vmem),
        scratch_shapes=[
            pltpu.VMEM((near, 2, half, 128), F32),
            pltpu.VMEM((gxs, 2, half, 128), jnp.int32),
            pltpu.VMEM((2, 1, 128), F32),
            pltpu.VMEM((2, near, 1, 128), F32),
            pltpu.VMEM((3, 2, gxs, half, 128), F32),
            pltpu.VMEM((count, 128, 128), BF),
            pltpu.VMEM((128, 2048), BF),
            pltpu.VMEM((2048, 128), BF),
            pltpu.VMEM((256, 2048), BF),
            pltpu.VMEM((x_length, 2048), BF),
            pltpu.VMEM((x_length, 2048), F32),
            pltpu.VMEM((1024, 128), F32),
            pltpu.VMEM((1024, 128), F32),
            pltpu.VMEM((count, 32, 128), BF),
            pltpu.VMEM((count, 32, 128), BF),
            pltpu.VMEM((count, 32, 128), BF),
            pltpu.VMEM((count, 32, 128), BF),
            pltpu.VMEM((count, 1, 128), F32),
            pltpu.VMEM((count, 1, 128), F32),
            pltpu.VMEM((1, 128), F32),
            dma((near,)),
            dma((near,)),
            dma((2,)),
            dma((2, near)),
            dma((2, near)),
        ]
        + [dma((count,))] * 8,
        compiler_params=pltpu.CompilerParams(
            collective_id=0, has_side_effects=True, vmem_limit_bytes=32 * 1024 * 1024
        ),
        cost_estimate=pl.CostEstimate(
            flops=400_000_000, bytes_accessed=2_000_000, transcendentals=200_000
        ),
    )(
        slot_field,
        solid,
        lift_weight,
        spectral_weight,
        mix_weight,
        project_weight,
        mode_index.reshape(1, -1),
    )
    mix_grad = jnp.transpose(mix_rows.reshape(32, 2, 64), (1, 0, 2)).reshape(64, 64)
    return (new_velocity, spectral_grad, mix_grad)


def local(slot_field, solid, lift_weight, spectral_weight, mix_weight, project_weight, mode_index):
    arrays = (slot_field, solid, lift_weight, spectral_weight, mix_weight, project_weight, mode_index)
    grps, gxs, gys = (lax.axis_size(axis) for axis in ("grp", "gx", "gy"))
    _, planes, x_rows, y_cols = slot_field.shape
    x_length = x_rows * gxs
    sizes = (grps, gxs, gys, x_length, x_length * y_cols * gys * planes)
    fits = (
        grps * gxs * gys == mode_index.shape[0] == 32
        and mix_weight.shape[0] == 64
        and gxs == planes == 2
        and y_cols == 32 * grps == 128
        and x_rows == 48
    )
    if fits:
        return fused(sizes, *arrays)
    return general(*arrays)


def solution(mesh):
    in_specs = (P("grp", None, "gx", "gy"), P(None, "gx", "gy"), P(), P(), P(), P(), P())
    out_specs = (P(None, None, "gx", "gy"), P(("grp", "gx", "gy"), None), P())
    return jax.shard_map(local, mesh=mesh, in_specs=in_specs, out_specs=out_specs, check_vma=False)
```

```python
import functools
import math

import jax
import jax.numpy as jnp
from jax import lax
from jax.experimental import pallas as pl
from jax.experimental.pallas import tpu as pltpu
from jax.sharding import PartitionSpec as P

VISCOSITY = 0.05
TIME_STEP = 0.1


def with_halo(block, sides, width):
    for axis, dim in sides:
        count = lax.axis_size(axis)
        forward = [(i, i + 1) for i in range(count - 1)]
        backward = [(target, source) for source, target in forward]
        low = lax.ppermute(
            lax.slice_in_dim(block, block.shape[dim] - width, None, axis=dim), axis, forward
        )
        high = lax.ppermute(lax.slice_in_dim(block, 0, width, axis=dim), axis, backward)
        block = jnp.concatenate([low, block, high], axis=dim)
    return block


def interior(source):
    return source[1:-1, 1:-1, 1:-1]


def along_x(source):
    return 0.5 * (source[1:-1, 2:, 1:-1] - source[1:-1, :-2, 1:-1])


def along_y(source):
    return 0.5 * (source[1:-1, 1:-1, 2:] - source[1:-1, 1:-1, :-2])


def along_z(source):
    return 0.5 * (source[2:, 1:-1, 1:-1] - source[:-2, 1:-1, 1:-1])


def laplace(source):
    total = source[2:, 1:-1, 1:-1] + source[:-2, 1:-1, 1:-1]
    total = total + source[1:-1, 2:, 1:-1] + source[1:-1, :-2, 1:-1]
    total = total + source[1:-1, 1:-1, 2:] + source[1:-1, 1:-1, :-2]
    return total - 6.0 * interior(source)


def section_component(padded, component, solid):
    source = padded[component]
    velocity = [interior(padded[index]) for index in range(3)]
    advect = (
        velocity[0] * along_x(source)
        + velocity[1] * along_y(source)
        + velocity[2] * along_z(source)
    )
    pressure = padded[3]
    press_grad = jnp.stack([along_x(pressure), along_y(pressure), along_z(pressure)])[component]
    update = interior(source) + TIME_STEP * (VISCOSITY * laplace(source) - advect - press_grad)
    return update * (1.0 - solid.astype(jnp.float32))


def spectral_table(mode_index, x_length):
    places = jnp.arange(x_length, dtype=jnp.int32)
    phases = mode_index[:, None] * places[None, :] % x_length
    angles = 2.0 * jnp.pi / x_length * phases.astype(jnp.float32)
    return jnp.concatenate([jnp.cos(angles), -jnp.sin(angles)], axis=0).astype(jnp.bfloat16)


def contract(form, left, right):
    return jnp.einsum(form, left, right, preferred_element_type=jnp.float32)


def student_terms(
    line_data,
    dft_table,
    lift_weight,
    spectral_weight,
    mix_weight,
    project_weight,
    loss_scale,
    x_length,
):
    mode_count = dft_table.shape[0] // 2
    chan_count = mix_weight.shape[0]
    scale_dft = 1.0 / math.sqrt(x_length)
    old_part = line_data[:3]
    target = line_data[3:].astype(jnp.float32)
    lifted = contract("iln,ic->cln", old_part, lift_weight).astype(jnp.bfloat16)
    coeffs = (contract("cln,mn->clm", lifted, dft_table) * scale_dft).astype(jnp.bfloat16)
    real_in = coeffs[..., :mode_count]
    imag_in = coeffs[..., mode_count:]
    weights = spectral_weight.reshape(mode_count, chan_count, 2 * chan_count)
    real_w = weights[..., :chan_count]
    imag_w = weights[..., chan_count:]
    real_out = contract("clm,mco->olm", real_in, real_w) - contract("clm,mco->olm", imag_in, imag_w)
    imag_out = contract("clm,mco->olm", real_in, imag_w) + contract("clm,mco->olm", imag_in, real_w)
    mixed = jnp.concatenate([real_out, imag_out], axis=2).astype(jnp.bfloat16)
    spectral = contract("olm,mn->oln", mixed, dft_table) * (2.0 * scale_dft)
    local_term = contract("cln,co->oln", lifted, mix_weight)
    hidden = spectral + local_term
    active, gelu_back = jax.vjp(jax.nn.gelu, hidden)
    active = active.astype(jnp.bfloat16)
    predicted = contract("oln,oi->iln", active, project_weight)
    misfit = (predicted - target) * loss_scale
    back_active = jnp.einsum(
        "iln,oi->oln", misfit, project_weight.astype(jnp.float32), precision=lax.Precision.HIGHEST
    )
    back_hidden = gelu_back(back_active)[0].astype(jnp.bfloat16)
    mix_part = contract("cln,oln->co", lifted, back_hidden)
    back_mixed = (contract("oln,mn->olm", back_hidden, dft_table) * (2.0 * scale_dft)).astype(
        jnp.bfloat16
    )
    back_real = back_mixed[..., :mode_count]
    back_imag = back_mixed[..., mode_count:]
    grad_real = contract("clm,olm->mco", real_in, back_real) + contract(
        "clm,olm->mco", imag_in, back_imag
    )
    grad_imag = contract("clm,olm->mco", real_in, back_imag) - contract(
        "clm,olm->mco", imag_in, back_real
    )
    spectral_part = jnp.concatenate([grad_real, grad_imag], axis=2).reshape(
        mode_count * chan_count, 2 * chan_count
    )
    return (spectral_part, mix_part)


def general(slot_field, solid, lift_weight, spectral_weight, mix_weight, project_weight, mode_index):
    role_index = lax.axis_index("grp")
    own_tile = slot_field[0]
    planes, x_rows, y_cols = own_tile.shape
    x_length = x_rows * lax.axis_size("gx")
    cell_total = x_length * y_cols * lax.axis_size("gy") * planes
    loss_scale = 16.0 / math.sqrt(cell_total)
    dft_table = spectral_table(mode_index, x_length)
    rimmed = with_halo(own_tile, (("gx", 1), ("gy", 2)), 1)
    gathered = lax.all_gather(rimmed[None], "grp", axis=0, tiled=True)
    padded = jnp.pad(gathered, ((0, 0), (1, 1), (0, 0), (0, 0)))
    old_velocity = gathered[:3, :, 1:-1, 1:-1]
    new_tile = lax.cond(
        role_index < 3,
        lambda: section_component(padded, jnp.minimum(role_index, 2), solid),
        lambda: own_tile,
    )
    new_slots = lax.all_gather(new_tile[None], "grp", axis=0, tiled=True)
    new_velocity = new_slots[:3]
    both_fields = jnp.concatenate([old_velocity, new_velocity], axis=0).astype(jnp.bfloat16)
    pencil_data = lax.all_to_all(
        jnp.transpose(both_fields, (0, 1, 3, 2)), "gx", split_axis=2, concat_axis=3, tiled=True
    )
    line_data = pencil_data.reshape(6, -1, x_length)

    def student(own_lines):
        return student_terms(
            own_lines,
            dft_table,
            lift_weight,
            spectral_weight,
            mix_weight,
            project_weight,
            loss_scale,
            x_length,
        )

    def nothing():
        return (
            jnp.zeros(spectral_weight.shape, jnp.float32),
            jnp.zeros(mix_weight.shape, jnp.float32),
        )

    spectral_part, mix_part = lax.cond(role_index == 3, lambda: student(line_data), nothing)
    spectral_grad = lax.psum_scatter(
        spectral_part, ("grp", "gx", "gy"), scatter_dimension=0, tiled=True
    )
    mix_grad = lax.psum(mix_part, ("grp", "gx", "gy"))
    return (new_velocity, spectral_grad, mix_grad)


MESH = pl.DeviceIdType.MESH
BF = jnp.bfloat16
F32 = jnp.float32


def dot(left, right, contract_dims=((1,), (0,))):
    return lax.dot_general(left, right, (contract_dims, ((), ())), preferred_element_type=F32)


def iota(shape, dim):
    return lax.broadcasted_iota(jnp.int32, shape, dim)


def fused_kernel(
    sizes,
    field_ref,
    solid_ref,
    lift_ref,
    spec_ref,
    mix_ref,
    proj_ref,
    mode_ref,
    newv_ref,
    grad_ref,
    mixg_ref,
    spec_vm,
    gath,
    both_solid,
    edge,
    rims,
    fresh,
    wide_mix,
    lift_big,
    proj_down,
    proj_up,
    lifted_ref,
    slope_ref,
    stage,
    stage_out,
    a_own,
    d_own,
    a_all,
    d_all,
    m_part,
    m_recv,
    m_row,
    m_all,
    load,
    field_send,
    field_recv,
    solid_sem,
    rim_send,
    rim_recv,
    a_sems,
    d_sems_a,
    d_sems_b,
    m_sems,
    r_sems,
):
    grps, gxs, gys, x_length, cell_total = sizes
    count = grps * gxs * gys
    near = grps * gxs
    half = x_length // gxs
    modes = count
    lines = 32
    pairs = lines // 2
    chans = 64
    g = lax.axis_index("grp")
    gx = lax.axis_index("gx")
    gy = lax.axis_index("gy")
    me = (g * gxs + gx) * gys + gy
    slot = g * gxs + gx
    scale_dft = 1.0 / math.sqrt(x_length)
    loss_scale = 16.0 / math.sqrt(cell_total)
    d_sems = (d_sems_a, d_sems_b)

    g_at = [(g + d) % grps for d in range(grps)]
    x_at = [(gx + d) % gxs for d in range(gxs)]
    y_at = [(gy + d) % gys for d in range(gys)]
    peers = []
    for dy in [gys // 2] + [d for d in range(gys) if d != gys // 2]:
        for dg in range(grps):
            for dx in range(gxs):
                if (dg, dx, dy) != (0, 0, 0):
                    place = {"grp": g_at[dg], "gx": x_at[dx], "gy": y_at[dy]}
                    peers.append((place, (g_at[dg] * gxs + x_at[dx]) * gys + y_at[dy]))

    barrier = pltpu.get_barrier_semaphore()
    for place, _ in peers:
        pl.semaphore_signal(barrier, inc=1, device_id=place, device_id_type=MESH)

    loads = [
        pltpu.make_async_copy(field_ref.at[0], gath.at[slot], load.at[0]),
        pltpu.make_async_copy(solid_ref, both_solid.at[gx], load.at[1]),
        pltpu.make_async_copy(spec_ref, spec_vm, load.at[2]),
    ]
    for copy in loads:
        copy.start()
    loads[0].wait()

    own = gath[pl.ds(slot, 1)][0]
    flat = jnp.concatenate([own.reshape(2 * half, 128), jnp.zeros((128 - 2 * half, 128), F32)], axis=0)
    turned = jnp.transpose(flat)
    edge[0] = turned[0:1, :]
    edge[1] = turned[127:128, :]

    @pl.when(gy == 0)
    def _():
        rims[0] = jnp.zeros((near, 1, 128), F32)

    @pl.when(gy == gys - 1)
    def _():
        rims[1] = jnp.zeros((near, 1, 128), F32)

    pl.semaphore_wait(barrier, count - 1)

    near_peers = []
    for dg in range(grps):
        for dx in range(gxs):
            if (dg, dx) != (0, 0):
                place = {"grp": g_at[dg], "gx": x_at[dx], "gy": gy}
                near_peers.append((place, g_at[dg] * gxs + x_at[dx]))

    def field_copy(place, s, at):
        return pltpu.make_async_remote_copy(
            src_ref=field_ref.at[0],
            dst_ref=gath.at[at],
            send_sem=field_send.at[s],
            recv_sem=field_recv.at[at],
            device_id=place,
            device_id_type=MESH,
        )

    def rim_copy(side, s, at):
        return pltpu.make_async_remote_copy(
            src_ref=edge.at[side],
            dst_ref=rims.at[1 - side, at],
            send_sem=rim_send.at[side, s],
            recv_sem=rim_recv.at[1 - side, at],
            device_id={"grp": s // gxs, "gx": s % gxs, "gy": gy - 1 + 2 * side},
            device_id_type=MESH,
        )

    def each_near(body):
        def step(s, carry):
            body(s)
            return carry

        lax.fori_loop(0, near, step, 0)

    for place, s in near_peers:
        field_copy(place, s, slot).start()

    @pl.when(gy > 0)
    def _():
        each_near(lambda s: rim_copy(0, s, slot).start())

    @pl.when(gy < gys - 1)
    def _():
        each_near(lambda s: rim_copy(1, s, slot).start())

    solid_copy = pltpu.make_async_remote_copy(
        src_ref=solid_ref,
        dst_ref=both_solid.at[gx],
        send_sem=solid_sem.at[0],
        recv_sem=solid_sem.at[1],
        device_id={"grp": g, "gx": x_at[1], "gy": gy},
        device_id_type=MESH,
    )
    solid_copy.start()
    for copy in loads[1:]:
        copy.wait()

    lane = iota((x_length, 128), 1)
    low16 = iota((16, 128), 1) < 64
    mode_row = mode_ref[...].astype(F32)
    mode_row = jnp.concatenate([mode_row] * 4, axis=1)
    place = iota((x_length, 128), 0).astype(F32)
    raw = mode_row * place + jnp.where(lane >= modes, 0.25 * x_length, 0.0)
    phase = raw - x_length * jnp.floor((raw + 0.5) * (1.0 / x_length))
    phase = jnp.where(phase >= 0.5 * x_length, phase - x_length, phase)
    angle = phase * (math.pi / x_length)
    square = angle * angle
    series = jnp.full_like(square, -1.0 / 39916800.0)
    for term in (1.0 / 362880.0, -1.0 / 5040.0, 1.0 / 120.0, -1.0 / 6.0, 1.0):
        series = series * square + term
    sine = series * angle
    waves = 1.0 - 2.0 * sine * sine
    table_t = waves[:, : 2 * modes].astype(BF)
    table = jnp.transpose(jnp.concatenate([waves, jnp.zeros((128 - x_length, 128), F32)], axis=0))
    table = table[: 2 * modes, :x_length].astype(BF)

    row128 = iota((128, 128), 0)
    col128 = iota((128, 128), 1)
    lift = lift_ref[...].astype(F32)
    lift = jnp.concatenate([lift, lift], axis=1)
    lift_rows = jnp.where(
        row128 < 32,
        lift[0:1],
        jnp.where(row128 < 64, lift[1:2], jnp.where(row128 < 96, lift[2:3], 0.0)),
    )
    proj = proj_ref[...].astype(F32)
    proj = jnp.concatenate([proj, proj], axis=1)
    proj_rows = jnp.where(
        row128 < 32,
        proj[0:1],
        jnp.where(row128 < 64, proj[1:2], jnp.where(row128 < 96, proj[2:3], 0.0)),
    )
    proj_cols = jnp.transpose(proj_rows)[:64]
    col64 = iota((64, 128), 1)
    line_of_row = jnp.bitwise_and(row128, 31)
    half_of_lane = jnp.where(col128 < 64, 0, 1)
    line_of_col = jnp.bitwise_and(col64, 31)

    def widen(p, carry):
        hit = line_of_row == 2 * p + half_of_lane
        cols = pl.ds(pl.multiple_of(p * 128, 128), 128)
        lift_big[:, cols] = jnp.where(hit, lift_rows, 0.0).astype(BF)
        up = jnp.where(hit, proj_rows, 0.0).astype(BF)
        proj_up[0:128, cols] = up
        proj_up[128:256, cols] = up
        for part in range(2):
            down = jnp.where(line_of_col == 2 * p + part, proj_cols, 0.0).astype(BF)
            proj_down[pl.ds(pl.multiple_of(p * 128 + part * 64, 64), 64), :] = down
        return carry

    lax.fori_loop(0, pairs, widen, 0)

    low_half = col64 < 64

    def widen_mix(m, carry):
        block = spec_vm[pl.ds(pl.multiple_of(m * 64, 64), 64), :]
        wide = block.astype(F32)
        turned_block = pltpu.roll(wide, 64, 1)
        wide_mix[m, 0:64, :] = block
        wide_mix[m, 64:128, :] = jnp.where(low_half, -turned_block, turned_block).astype(BF)
        return carry

    lax.fori_loop(0, modes, widen_mix, 0)

    mix = mix_ref[...].astype(F32)
    mix = jnp.concatenate([mix, mix], axis=1)
    mix = jnp.concatenate([mix, mix], axis=0)
    mix = jnp.where((row128 < 64) == (col128 < 64), mix, 0.0)
    blank = jnp.zeros_like(mix)
    mix_four = jnp.concatenate(
        [jnp.concatenate([mix, blank], axis=1), jnp.concatenate([blank, mix], axis=1)], axis=0
    ).astype(BF)
    pick = jnp.concatenate(
        [
            jnp.where((col128 // 32 == i) & (row128 == 32 * g + jnp.bitwise_and(col128, 31)), 1.0, 0.0)
            for i in range(3)
        ],
        axis=0,
    ).astype(BF)

    for place, s in near_peers:
        field_copy(place, s, s).wait_recv()
    solid_copy.wait_recv()

    @pl.when(gy > 0)
    def _():
        each_near(lambda s: rim_copy(1, s, s).wait_recv())

    @pl.when(gy < gys - 1)
    def _():
        each_near(lambda s: rim_copy(0, s, s).wait_recv())

    rim_rows = [rims[side, s] for side in range(2) for s in range(near)]
    rim_rows.append(jnp.zeros((128 - 2 * near, 128), F32))
    rim_cols = jnp.transpose(jnp.concatenate(rim_rows, axis=0))
    first_row = iota((x_length, 128), 0) == 0
    last_row = iota((x_length, 128), 0) == x_length - 1

    def whole(f, z):
        return jnp.concatenate([gath[f * gxs + h, z] for h in range(gxs)], axis=0)

    def rim(f, z, side):
        cols = [
            rim_cols[z * half : (z + 1) * half, side * near + f * gxs + h :][:, 0:1] for h in range(gxs)
        ]
        return jnp.concatenate(cols, axis=0)

    def shifted(f, z, value):
        x_up = jnp.where(last_row, 0.0, pltpu.roll(value, x_length - 1, 0))
        x_down = jnp.where(first_row, 0.0, pltpu.roll(value, 1, 0))
        y_up = jnp.where(lane == 127, rim(f, z, 1), pltpu.roll(value, 127, 1))
        y_down = jnp.where(lane == 0, rim(f, z, 0), pltpu.roll(value, 1, 1))
        return x_up, x_down, y_up, y_down

    for z in range(2):
        fluid = 1.0 - jnp.concatenate([both_solid[h, z] for h in range(gxs)], axis=0).astype(F32)
        here = [whole(f, z) for f in range(4)]
        there = [whole(f, 1 - z) for f in range(4)]
        sign_z = 0.5 if z == 0 else -0.5
        press = shifted(3, z, here[3])
        grads = (0.5 * (press[0] - press[1]), 0.5 * (press[2] - press[3]), sign_z * there[3])
        for k in range(3):
            x_up, x_down, y_up, y_down = shifted(k, z, here[k])
            lap = there[k] + x_up + x_down + y_up + y_down - 6.0 * here[k]
            advect = (
                here[0] * (0.5 * (x_up - x_down))
                + here[1] * (0.5 * (y_up - y_down))
                + here[2] * (sign_z * there[k])
            )
            update = here[k] + TIME_STEP * (VISCOSITY * lap - advect - grads[k])
            update = update * fluid
            for h in range(gxs):
                fresh[h, k, z] = update[h * half : (h + 1) * half]
    result_copy = pltpu.make_async_copy(fresh.at[gx], newv_ref, load.at[3])
    result_copy.start()

    old = [jnp.concatenate([gath[i * gxs + h, gx] for h in range(gxs)], axis=0) for i in range(3)]
    new = [jnp.concatenate([fresh[h, i, gx] for h in range(gxs)], axis=0) for i in range(3)]
    stacked = jnp.concatenate([jnp.concatenate(old, axis=1), jnp.concatenate(new, axis=1)], axis=0)
    picked = dot(stacked.astype(BF), pick)
    source = picked[:x_length].astype(BF)
    target = picked[x_length:]

    for b in range(pairs // 2):
        cols = slice(b * 256, (b + 1) * 256)
        lifted = dot(source, lift_big[:, cols]).astype(BF)
        lifted_ref[:, cols] = lifted
        coeffs = dot(table, lifted) * scale_dft
        stage[2 * b * 64 : (2 * b + 1) * 64, :] = coeffs[:, :128]
        stage[(2 * b + 1) * 64 : (2 * b + 2) * 64, :] = coeffs[:, 128:]

    def mode_rows(m, rows_of, keep):
        real = stage[pl.ds(m, rows_of, stride=64), :]
        imag = stage[pl.ds(modes + m, rows_of, stride=64), :]
        low = iota((rows_of, 128), 1) < 64
        top = jnp.where(low, real, pltpu.roll(imag, 64, 1))
        bottom = jnp.where(low, pltpu.roll(real, 64, 1), imag)
        keep(jnp.concatenate([top[:8], bottom[:8], top[8:], bottom[8:]][: rows_of // 4], axis=0))

    def all_modes(body):
        def step(m, carry):
            body(m)
            return carry

        lax.fori_loop(0, modes, step, 0, unroll=8)

    def exchange(src, dst, sems, place, sent, landed):
        return pltpu.make_async_remote_copy(
            src_ref=src,
            dst_ref=dst,
            send_sem=sems.at[0, sent],
            recv_sem=sems.at[1, landed],
            device_id=place,
            device_id_type=MESH,
        )

    def a_copy(place, t, at):
        return exchange(a_own.at[t], a_all.at[at], a_sems, place, t, at)

    def d_copy(part, place, t, at):
        return exchange(d_own.at[part, t], d_all.at[part, at], d_sems[part], place, t, at)

    def m_copy(place, t, at):
        return exchange(m_part.at[t], m_recv.at[at], m_sems, place, t, at)

    def r_copy(place, t, at):
        return exchange(m_row, m_all.at[at], r_sems, place, t, at)

    def keep_a(m):
        def keep(rows):
            both = rows.astype(BF)
            a_own[m, 0] = both[:16]
            a_own[m, 1] = both[16:]

        mode_rows(m, pairs, keep)

    all_modes(keep_a)
    for place, t in peers:
        a_copy(place, t, me).start()
    a_all[pl.ds(me, 1)] = a_own[pl.ds(me, 1)]

    def mix_mode(m):
        out = dot(a_own[m].reshape(lines, 2 * chans), wide_mix[m])
        top = jnp.concatenate([out[:8], out[16:24]], axis=0)
        bottom = jnp.concatenate([out[8:16], out[24:]], axis=0)
        stage_out[pl.ds(m, pairs, stride=64), :] = jnp.where(
            low16, top, pltpu.roll(bottom, 64, 1)
        )
        stage_out[pl.ds(modes + m, pairs, stride=64), :] = jnp.where(
            low16, pltpu.roll(top, 64, 1), bottom
        )

    all_modes(mix_mode)

    root = math.sqrt(2.0 / math.pi)
    mix_sum = jnp.zeros((128, 128), F32)
    for half_lines in range(2):
        blocks = range(half_lines * 4, half_lines * 4 + 4)
        predicted = jnp.zeros((x_length, 128), F32)
        for b in blocks:
            cols = slice(b * 256, (b + 1) * 256)
            mixed = jnp.concatenate(
                [
                    stage_out[2 * b * 64 : (2 * b + 1) * 64, :],
                    stage_out[(2 * b + 1) * 64 : (2 * b + 2) * 64, :],
                ],
                axis=1,
            ).astype(BF)
            hidden = dot(table_t, mixed) * (2.0 * scale_dft) + dot(lifted_ref[:, cols], mix_four)
            squared = hidden * hidden
            bent = jnp.tanh(root * hidden * (1.0 + 0.044715 * squared))
            upper = 0.5 * (1.0 + bent)
            active = (hidden * upper).astype(BF)
            slope_ref[:, cols] = upper + 0.5 * hidden * (1.0 - bent * bent) * (
                root * (1.0 + 3.0 * 0.044715 * squared)
            )
            predicted = predicted + dot(active, proj_down[b * 256 : (b + 1) * 256, :])
        misfit = (predicted - target) * loss_scale
        coarse = misfit.astype(BF)
        fine = (misfit - coarse.astype(F32)).astype(BF)
        misfit_parts = jnp.concatenate([coarse, fine], axis=1)
        for b in blocks:
            cols = slice(b * 256, (b + 1) * 256)
            back_active = dot(misfit_parts, proj_up[:, cols])
            back_hidden = (slope_ref[:, cols] * back_active).astype(BF)
            lifted = lifted_ref[:, cols]
            for part in range(2):
                lanes = slice(part * 128, (part + 1) * 128)
                mix_sum = mix_sum + dot(lifted[:, lanes], back_hidden[:, lanes], ((0,), (0,)))
            back = dot(table, back_hidden) * (2.0 * scale_dft)
            at = 2 * (b % 4) * 64
            stage[at : at + 64, :] = back[:, :128]
            stage[at + 64 : at + 128, :] = back[:, 128:]

        if half_lines == 1:
            mix_own = mix_sum[:64] + pltpu.roll(mix_sum[64:], 64, 1)
            packed = jnp.where(
                iota((32, 128), 1) < 64, mix_own[:32], pltpu.roll(mix_own[32:], 64, 1)
            )
            for row in range(count):
                m_part[row] = packed[row : row + 1, :]
            for place, t in peers:
                m_copy(place, t, me).start()
            m_recv[pl.ds(me, 1)] = m_part[pl.ds(me, 1)]

        def keep_d(m):
            def keep(rows):
                d_own[half_lines, m] = rows.astype(BF)

            mode_rows(m, pairs // 2, keep)

        all_modes(keep_d)
        for place, t in peers:
            d_copy(half_lines, place, t, me).start()
        d_all[half_lines, pl.ds(me, 1)] = d_own[half_lines, pl.ds(me, 1)]

    for place, t in peers:
        m_copy(place, t, t).wait_recv()
    total = jnp.sum(m_recv[...], axis=0)
    m_row[...] = total
    m_all[pl.ds(me, 1)] = total[None]
    for place, t in peers:
        r_copy(place, t, me).start()

    for place, t in peers:
        a_copy(place, t, t).wait_recv()
    square_sum = jnp.zeros((128, 128), F32)
    for half_lines in range(2):
        for place, t in peers:
            d_copy(half_lines, place, t, t).wait_recv()
        a_lines = a_all[:, half_lines].reshape(count * 16, 2 * chans)
        d_lines = d_all[half_lines].reshape(count * 16, 2 * chans)
        square_sum = square_sum + dot(a_lines, d_lines, ((0,), (0,)))
    turned_sum = pltpu.roll(square_sum[64:], 64, 1)
    grad_ref[...] = square_sum[:64] + jnp.where(low_half, turned_sum, -turned_sum)

    for place, t in peers:
        r_copy(place, t, t).wait_recv()
    rows = jnp.concatenate([m_all[row] for row in range(count)], axis=0)
    mixg_ref[...] = jnp.concatenate([rows[:, :64], rows[:, 64:]], axis=0)

    result_copy.wait()
    for place, s in near_peers:
        field_copy(place, s, slot).wait_send()
    solid_copy.wait_send()

    @pl.when(gy > 0)
    def _():
        each_near(lambda s: rim_copy(0, s, slot).wait_send())

    @pl.when(gy < gys - 1)
    def _():
        each_near(lambda s: rim_copy(1, s, slot).wait_send())

    for place, t in peers:
        a_copy(place, t, me).wait_send()
        d_copy(0, place, t, me).wait_send()
        d_copy(1, place, t, me).wait_send()
        m_copy(place, t, me).wait_send()
        r_copy(place, t, me).wait_send()


def fused(sizes, slot_field, solid, lift_weight, spectral_weight, mix_weight, project_weight, mode_index):
    grps, gxs, gys, x_length, _ = sizes
    count = grps * gxs * gys
    near = grps * gxs
    half = x_length // gxs
    dma = pltpu.SemaphoreType.DMA
    vmem = pl.BlockSpec(memory_space=pltpu.VMEM)
    whole = pl.BlockSpec(memory_space=pl.ANY)
    shape = jax.ShapeDtypeStruct
    return pl.pallas_call(
        functools.partial(fused_kernel, sizes),
        out_shape=(
            shape((3, 2, half, 128), F32),
            shape((64, 128), F32),
            shape((64, 64), F32),
        ),
        in_specs=[whole, whole, vmem, whole, vmem, vmem, vmem],
        out_specs=(whole, vmem, vmem),
        scratch_shapes=[
            pltpu.VMEM((64 * count, 128), BF),
            pltpu.VMEM((near, 2, half, 128), F32),
            pltpu.VMEM((gxs, 2, half, 128), jnp.int32),
            pltpu.VMEM((2, 1, 128), F32),
            pltpu.VMEM((2, near, 1, 128), F32),
            pltpu.VMEM((gxs, 3, 2, half, 128), F32),
            pltpu.VMEM((count, 128, 128), BF),
            pltpu.VMEM((128, 2048), BF),
            pltpu.VMEM((2048, 128), BF),
            pltpu.VMEM((256, 2048), BF),
            pltpu.VMEM((x_length, 2048), BF),
            pltpu.VMEM((x_length, 2048), F32),
            pltpu.VMEM((1024, 128), F32),
            pltpu.VMEM((1024, 128), F32),
            pltpu.VMEM((count, 2, 16, 128), BF),
            pltpu.VMEM((2, count, 16, 128), BF),
            pltpu.VMEM((count, 2, 16, 128), BF),
            pltpu.VMEM((2, count, 16, 128), BF),
            pltpu.VMEM((count, 1, 128), F32),
            pltpu.VMEM((count, 1, 128), F32),
            pltpu.VMEM((1, 128), F32),
            pltpu.VMEM((count, 1, 128), F32),
            dma((4,)),
            dma((near,)),
            dma((near,)),
            dma((2,)),
            dma((2, near)),
            dma((2, near)),
        ]
        + [dma((2, count))] * 5,
        compiler_params=pltpu.CompilerParams(
            collective_id=0, has_side_effects=True, vmem_limit_bytes=60 * 1024 * 1024
        ),
        cost_estimate=pl.CostEstimate(
            flops=400_000_000, bytes_accessed=2_000_000, transcendentals=200_000
        ),
    )(
        slot_field,
        solid,
        lift_weight,
        spectral_weight,
        mix_weight,
        jnp.transpose(project_weight),
        mode_index.reshape(1, -1),
    )


def local(slot_field, solid, lift_weight, spectral_weight, mix_weight, project_weight, mode_index):
    arrays = (slot_field, solid, lift_weight, spectral_weight, mix_weight, project_weight, mode_index)
    grps, gxs, gys = (lax.axis_size(axis) for axis in ("grp", "gx", "gy"))
    _, planes, x_rows, y_cols = slot_field.shape
    x_length = x_rows * gxs
    sizes = (grps, gxs, gys, x_length, x_length * y_cols * gys * planes)
    fits = (
        grps * gxs * gys == mode_index.shape[0] == 32
        and mix_weight.shape[0] == 64
        and gxs == planes == 2
        and y_cols == 32 * grps == 128
        and x_rows == 48
    )
    if fits:
        return fused(sizes, *arrays)
    return general(*arrays)


def solution(mesh):
    in_specs = (P("grp", None, "gx", "gy"), P(None, "gx", "gy"), P(), P(), P(), P(), P())
    out_specs = (P(None, None, "gx", "gy"), P(("grp", "gx", "gy"), None), P())
    return jax.shard_map(local, mesh=mesh, in_specs=in_specs, out_specs=out_specs, check_vma=False)
```

```python
import functools
import math

import jax
import jax.numpy as jnp
from jax import lax
from jax.experimental import pallas as pl
from jax.experimental.pallas import tpu as pltpu
from jax.sharding import PartitionSpec as P

VISCOSITY = 0.05
TIME_STEP = 0.1


def with_halo(block, sides, width):
    for axis, dim in sides:
        count = lax.axis_size(axis)
        forward = [(i, i + 1) for i in range(count - 1)]
        backward = [(target, source) for source, target in forward]
        low = lax.ppermute(
            lax.slice_in_dim(block, block.shape[dim] - width, None, axis=dim), axis, forward
        )
        high = lax.ppermute(lax.slice_in_dim(block, 0, width, axis=dim), axis, backward)
        block = jnp.concatenate([low, block, high], axis=dim)
    return block


def interior(source):
    return source[1:-1, 1:-1, 1:-1]


def along_x(source):
    return 0.5 * (source[1:-1, 2:, 1:-1] - source[1:-1, :-2, 1:-1])


def along_y(source):
    return 0.5 * (source[1:-1, 1:-1, 2:] - source[1:-1, 1:-1, :-2])


def along_z(source):
    return 0.5 * (source[2:, 1:-1, 1:-1] - source[:-2, 1:-1, 1:-1])


def laplace(source):
    total = source[2:, 1:-1, 1:-1] + source[:-2, 1:-1, 1:-1]
    total = total + source[1:-1, 2:, 1:-1] + source[1:-1, :-2, 1:-1]
    total = total + source[1:-1, 1:-1, 2:] + source[1:-1, 1:-1, :-2]
    return total - 6.0 * interior(source)


def section_component(padded, component, solid):
    source = padded[component]
    velocity = [interior(padded[index]) for index in range(3)]
    advect = (
        velocity[0] * along_x(source)
        + velocity[1] * along_y(source)
        + velocity[2] * along_z(source)
    )
    pressure = padded[3]
    press_grad = jnp.stack([along_x(pressure), along_y(pressure), along_z(pressure)])[component]
    update = interior(source) + TIME_STEP * (VISCOSITY * laplace(source) - advect - press_grad)
    return update * (1.0 - solid.astype(jnp.float32))


def spectral_table(mode_index, x_length):
    places = jnp.arange(x_length, dtype=jnp.int32)
    phases = mode_index[:, None] * places[None, :] % x_length
    angles = 2.0 * jnp.pi / x_length * phases.astype(jnp.float32)
    return jnp.concatenate([jnp.cos(angles), -jnp.sin(angles)], axis=0).astype(jnp.bfloat16)


def contract(form, left, right):
    return jnp.einsum(form, left, right, preferred_element_type=jnp.float32)


def student_terms(
    line_data,
    dft_table,
    lift_weight,
    spectral_weight,
    mix_weight,
    project_weight,
    loss_scale,
    x_length,
):
    mode_count = dft_table.shape[0] // 2
    chan_count = mix_weight.shape[0]
    scale_dft = 1.0 / math.sqrt(x_length)
    old_part = line_data[:3]
    target = line_data[3:].astype(jnp.float32)
    lifted = contract("iln,ic->cln", old_part, lift_weight).astype(jnp.bfloat16)
    coeffs = (contract("cln,mn->clm", lifted, dft_table) * scale_dft).astype(jnp.bfloat16)
    real_in = coeffs[..., :mode_count]
    imag_in = coeffs[..., mode_count:]
    weights = spectral_weight.reshape(mode_count, chan_count, 2 * chan_count)
    real_w = weights[..., :chan_count]
    imag_w = weights[..., chan_count:]
    real_out = contract("clm,mco->olm", real_in, real_w) - contract("clm,mco->olm", imag_in, imag_w)
    imag_out = contract("clm,mco->olm", real_in, imag_w) + contract("clm,mco->olm", imag_in, real_w)
    mixed = jnp.concatenate([real_out, imag_out], axis=2).astype(jnp.bfloat16)
    spectral = contract("olm,mn->oln", mixed, dft_table) * (2.0 * scale_dft)
    local_term = contract("cln,co->oln", lifted, mix_weight)
    hidden = spectral + local_term
    active, gelu_back = jax.vjp(jax.nn.gelu, hidden)
    active = active.astype(jnp.bfloat16)
    predicted = contract("oln,oi->iln", active, project_weight)
    misfit = (predicted - target) * loss_scale
    back_active = jnp.einsum(
        "iln,oi->oln", misfit, project_weight.astype(jnp.float32), precision=lax.Precision.HIGHEST
    )
    back_hidden = gelu_back(back_active)[0].astype(jnp.bfloat16)
    mix_part = contract("cln,oln->co", lifted, back_hidden)
    back_mixed = (contract("oln,mn->olm", back_hidden, dft_table) * (2.0 * scale_dft)).astype(
        jnp.bfloat16
    )
    back_real = back_mixed[..., :mode_count]
    back_imag = back_mixed[..., mode_count:]
    grad_real = contract("clm,olm->mco", real_in, back_real) + contract(
        "clm,olm->mco", imag_in, back_imag
    )
    grad_imag = contract("clm,olm->mco", real_in, back_imag) - contract(
        "clm,olm->mco", imag_in, back_real
    )
    spectral_part = jnp.concatenate([grad_real, grad_imag], axis=2).reshape(
        mode_count * chan_count, 2 * chan_count
    )
    return (spectral_part, mix_part)


def general(slot_field, solid, lift_weight, spectral_weight, mix_weight, project_weight, mode_index):
    role_index = lax.axis_index("grp")
    own_tile = slot_field[0]
    planes, x_rows, y_cols = own_tile.shape
    x_length = x_rows * lax.axis_size("gx")
    cell_total = x_length * y_cols * lax.axis_size("gy") * planes
    loss_scale = 16.0 / math.sqrt(cell_total)
    dft_table = spectral_table(mode_index, x_length)
    rimmed = with_halo(own_tile, (("gx", 1), ("gy", 2)), 1)
    gathered = lax.all_gather(rimmed[None], "grp", axis=0, tiled=True)
    padded = jnp.pad(gathered, ((0, 0), (1, 1), (0, 0), (0, 0)))
    old_velocity = gathered[:3, :, 1:-1, 1:-1]
    new_tile = lax.cond(
        role_index < 3,
        lambda: section_component(padded, jnp.minimum(role_index, 2), solid),
        lambda: own_tile,
    )
    new_slots = lax.all_gather(new_tile[None], "grp", axis=0, tiled=True)
    new_velocity = new_slots[:3]
    both_fields = jnp.concatenate([old_velocity, new_velocity], axis=0).astype(jnp.bfloat16)
    pencil_data = lax.all_to_all(
        jnp.transpose(both_fields, (0, 1, 3, 2)), "gx", split_axis=2, concat_axis=3, tiled=True
    )
    line_data = pencil_data.reshape(6, -1, x_length)

    def student(own_lines):
        return student_terms(
            own_lines,
            dft_table,
            lift_weight,
            spectral_weight,
            mix_weight,
            project_weight,
            loss_scale,
            x_length,
        )

    def nothing():
        return (
            jnp.zeros(spectral_weight.shape, jnp.float32),
            jnp.zeros(mix_weight.shape, jnp.float32),
        )

    spectral_part, mix_part = lax.cond(role_index == 3, lambda: student(line_data), nothing)
    spectral_grad = lax.psum_scatter(
        spectral_part, ("grp", "gx", "gy"), scatter_dimension=0, tiled=True
    )
    mix_grad = lax.psum(mix_part, ("grp", "gx", "gy"))
    return (new_velocity, spectral_grad, mix_grad)


MESH = pl.DeviceIdType.MESH
BF = jnp.bfloat16
F32 = jnp.float32


def dot(left, right, contract_dims=((1,), (0,))):
    return lax.dot_general(left, right, (contract_dims, ((), ())), preferred_element_type=F32)


def iota(shape, dim):
    return lax.broadcasted_iota(jnp.int32, shape, dim)


def fused_kernel(
    sizes,
    field_ref,
    solid_ref,
    lift_ref,
    spec_ref,
    mix_ref,
    proj_ref,
    mode_ref,
    newv_ref,
    grad_ref,
    mixg_ref,
    spec_vm,
    gath,
    both_solid,
    edge,
    rims,
    fresh,
    wide_mix,
    lift_big,
    proj_down,
    proj_up,
    lifted_ref,
    slope_ref,
    stage,
    stage_out,
    a_own,
    d_own,
    a_all,
    d_all,
    m_part,
    m_recv,
    m_row,
    m_all,
    g_part,
    g_recv,
    load,
    field_send,
    field_recv,
    solid_sem,
    rim_send,
    rim_recv,
    a_sems,
    d_sems_a,
    d_sems_b,
    m_sems,
    r_sems,
    g_sems,
):
    grps, gxs, gys, x_length, cell_total = sizes
    count = grps * gxs * gys
    near = grps * gxs
    half = x_length // gxs
    modes = count
    lines = 32
    pairs = lines // 2
    chans = 64
    g = lax.axis_index("grp")
    gx = lax.axis_index("gx")
    gy = lax.axis_index("gy")
    me = (g * gxs + gx) * gys + gy
    slot = g * gxs + gx
    scale_dft = 1.0 / math.sqrt(x_length)
    loss_scale = 16.0 / math.sqrt(cell_total)
    d_sems = (d_sems_a, d_sems_b)

    g_at = [(g + d) % grps for d in range(grps)]
    x_at = [(gx + d) % gxs for d in range(gxs)]
    y_at = [(gy + d) % gys for d in range(gys)]
    peers = []
    for dy in [gys // 2] + [d for d in range(gys) if d != gys // 2]:
        for dg in range(grps):
            for dx in range(gxs):
                if (dg, dx, dy) != (0, 0, 0):
                    place = {"grp": g_at[dg], "gx": x_at[dx], "gy": y_at[dy]}
                    peers.append((place, (g_at[dg] * gxs + x_at[dx]) * gys + y_at[dy]))

    barrier = pltpu.get_barrier_semaphore()
    for place, _ in peers:
        pl.semaphore_signal(barrier, inc=1, device_id=place, device_id_type=MESH)

    loads = [
        pltpu.make_async_copy(field_ref.at[0], gath.at[slot], load.at[0]),
        pltpu.make_async_copy(solid_ref, both_solid.at[gx], load.at[1]),
        pltpu.make_async_copy(spec_ref, spec_vm, load.at[2]),
    ]
    for copy in loads:
        copy.start()
    loads[0].wait()

    own = gath[pl.ds(slot, 1)][0]
    flat = jnp.concatenate([own.reshape(2 * half, 128), jnp.zeros((128 - 2 * half, 128), F32)], axis=0)
    turned = jnp.transpose(flat)
    edge[0] = turned[0:1, :]
    edge[1] = turned[127:128, :]

    @pl.when(gy == 0)
    def _():
        rims[0] = jnp.zeros((near, 1, 128), F32)

    @pl.when(gy == gys - 1)
    def _():
        rims[1] = jnp.zeros((near, 1, 128), F32)

    pl.semaphore_wait(barrier, count - 1)

    near_peers = []
    for dg in range(grps):
        for dx in range(gxs):
            if (dg, dx) != (0, 0):
                place = {"grp": g_at[dg], "gx": x_at[dx], "gy": gy}
                near_peers.append((place, g_at[dg] * gxs + x_at[dx]))

    def field_copy(place, s, at):
        return pltpu.make_async_remote_copy(
            src_ref=field_ref.at[0],
            dst_ref=gath.at[at],
            send_sem=field_send.at[s],
            recv_sem=field_recv.at[at],
            device_id=place,
            device_id_type=MESH,
        )

    def rim_copy(side, s, at):
        return pltpu.make_async_remote_copy(
            src_ref=edge.at[side],
            dst_ref=rims.at[1 - side, at],
            send_sem=rim_send.at[side, s],
            recv_sem=rim_recv.at[1 - side, at],
            device_id={"grp": s // gxs, "gx": s % gxs, "gy": gy - 1 + 2 * side},
            device_id_type=MESH,
        )

    def each_near(body):
        def step(s, carry):
            body(s)
            return carry

        lax.fori_loop(0, near, step, 0)

    for place, s in near_peers:
        field_copy(place, s, slot).start()

    @pl.when(gy > 0)
    def _():
        each_near(lambda s: rim_copy(0, s, slot).start())

    @pl.when(gy < gys - 1)
    def _():
        each_near(lambda s: rim_copy(1, s, slot).start())

    solid_copy = pltpu.make_async_remote_copy(
        src_ref=solid_ref,
        dst_ref=both_solid.at[gx],
        send_sem=solid_sem.at[0],
        recv_sem=solid_sem.at[1],
        device_id={"grp": g, "gx": x_at[1], "gy": gy},
        device_id_type=MESH,
    )
    solid_copy.start()
    for copy in loads[1:]:
        copy.wait()

    lane = iota((x_length, 128), 1)
    low16 = iota((16, 128), 1) < 64
    mode_row = mode_ref[...].astype(F32)
    mode_row = jnp.concatenate([mode_row] * 4, axis=1)
    place = iota((x_length, 128), 0).astype(F32)
    raw = mode_row * place + jnp.where(lane >= modes, 0.25 * x_length, 0.0)
    phase = raw - x_length * jnp.floor((raw + 0.5) * (1.0 / x_length))
    phase = jnp.where(phase >= 0.5 * x_length, phase - x_length, phase)
    angle = phase * (math.pi / x_length)
    square = angle * angle
    series = jnp.full_like(square, -1.0 / 39916800.0)
    for term in (1.0 / 362880.0, -1.0 / 5040.0, 1.0 / 120.0, -1.0 / 6.0, 1.0):
        series = series * square + term
    sine = series * angle
    waves = 1.0 - 2.0 * sine * sine
    table_t = waves[:, : 2 * modes].astype(BF)
    table = jnp.transpose(jnp.concatenate([waves, jnp.zeros((128 - x_length, 128), F32)], axis=0))
    table = table[: 2 * modes, :x_length].astype(BF)

    row128 = iota((128, 128), 0)
    col128 = iota((128, 128), 1)
    lift = lift_ref[...].astype(F32)
    lift = jnp.concatenate([lift, lift], axis=1)
    lift_rows = jnp.where(
        row128 < 32,
        lift[0:1],
        jnp.where(row128 < 64, lift[1:2], jnp.where(row128 < 96, lift[2:3], 0.0)),
    )
    proj = proj_ref[...].astype(F32)
    proj = jnp.concatenate([proj, proj], axis=1)
    proj_rows = jnp.where(
        row128 < 32,
        proj[0:1],
        jnp.where(row128 < 64, proj[1:2], jnp.where(row128 < 96, proj[2:3], 0.0)),
    )
    proj_cols = jnp.transpose(proj_rows)[:64]
    col64 = iota((64, 128), 1)
    line_of_row = jnp.bitwise_and(row128, 31)
    half_of_lane = jnp.where(col128 < 64, 0, 1)
    line_of_col = jnp.bitwise_and(col64, 31)

    def widen(p, carry):
        hit = line_of_row == 2 * p + half_of_lane
        cols = pl.ds(pl.multiple_of(p * 128, 128), 128)
        lift_big[:, cols] = jnp.where(hit, lift_rows, 0.0).astype(BF)
        up = jnp.where(hit, proj_rows, 0.0).astype(BF)
        proj_up[0:128, cols] = up
        proj_up[128:256, cols] = up
        for part in range(2):
            down = jnp.where(line_of_col == 2 * p + part, proj_cols, 0.0).astype(BF)
            proj_down[pl.ds(pl.multiple_of(p * 128 + part * 64, 64), 64), :] = down
        return carry

    lax.fori_loop(0, pairs, widen, 0)

    low_half = col64 < 64

    def widen_mix(m, carry):
        block = spec_vm[pl.ds(pl.multiple_of(m * 64, 64), 64), :]
        wide = block.astype(F32)
        turned_block = pltpu.roll(wide, 64, 1)
        wide_mix[m, 0:64, :] = block
        wide_mix[m, 64:128, :] = jnp.where(low_half, -turned_block, turned_block).astype(BF)
        return carry

    lax.fori_loop(0, modes, widen_mix, 0)

    mix = mix_ref[...].astype(F32)
    mix = jnp.concatenate([mix, mix], axis=1)
    mix = jnp.concatenate([mix, mix], axis=0)
    mix = jnp.where((row128 < 64) == (col128 < 64), mix, 0.0)
    blank = jnp.zeros_like(mix)
    mix_four = jnp.concatenate(
        [jnp.concatenate([mix, blank], axis=1), jnp.concatenate([blank, mix], axis=1)], axis=0
    ).astype(BF)
    pick = jnp.concatenate(
        [
            jnp.where((col128 // 32 == i) & (row128 == 32 * g + jnp.bitwise_and(col128, 31)), 1.0, 0.0)
            for i in range(3)
        ],
        axis=0,
    ).astype(BF)

    for place, s in near_peers:
        field_copy(place, s, s).wait_recv()
    solid_copy.wait_recv()

    @pl.when(gy > 0)
    def _():
        each_near(lambda s: rim_copy(1, s, s).wait_recv())

    @pl.when(gy < gys - 1)
    def _():
        each_near(lambda s: rim_copy(0, s, s).wait_recv())

    rim_rows = [rims[side, s] for side in range(2) for s in range(near)]
    rim_rows.append(jnp.zeros((128 - 2 * near, 128), F32))
    rim_cols = jnp.transpose(jnp.concatenate(rim_rows, axis=0))
    first_row = iota((x_length, 128), 0) == 0
    last_row = iota((x_length, 128), 0) == x_length - 1

    def whole(f, z):
        return jnp.concatenate([gath[f * gxs + h, z] for h in range(gxs)], axis=0)

    def rim(f, z, side):
        cols = [
            rim_cols[z * half : (z + 1) * half, side * near + f * gxs + h :][:, 0:1] for h in range(gxs)
        ]
        return jnp.concatenate(cols, axis=0)

    def shifted(f, z, value):
        x_up = jnp.where(last_row, 0.0, pltpu.roll(value, x_length - 1, 0))
        x_down = jnp.where(first_row, 0.0, pltpu.roll(value, 1, 0))
        y_up = jnp.where(lane == 127, rim(f, z, 1), pltpu.roll(value, 127, 1))
        y_down = jnp.where(lane == 0, rim(f, z, 0), pltpu.roll(value, 1, 1))
        return x_up, x_down, y_up, y_down

    for z in range(2):
        fluid = 1.0 - jnp.concatenate([both_solid[h, z] for h in range(gxs)], axis=0).astype(F32)
        here = [whole(f, z) for f in range(4)]
        there = [whole(f, 1 - z) for f in range(4)]
        sign_z = 0.5 if z == 0 else -0.5
        press = shifted(3, z, here[3])
        grads = (0.5 * (press[0] - press[1]), 0.5 * (press[2] - press[3]), sign_z * there[3])
        for k in range(3):
            x_up, x_down, y_up, y_down = shifted(k, z, here[k])
            lap = there[k] + x_up + x_down + y_up + y_down - 6.0 * here[k]
            advect = (
                here[0] * (0.5 * (x_up - x_down))
                + here[1] * (0.5 * (y_up - y_down))
                + here[2] * (sign_z * there[k])
            )
            update = here[k] + TIME_STEP * (VISCOSITY * lap - advect - grads[k])
            update = update * fluid
            for h in range(gxs):
                fresh[h, k, z] = update[h * half : (h + 1) * half]
    result_copy = pltpu.make_async_copy(fresh.at[gx], newv_ref, load.at[3])
    result_copy.start()

    old = [jnp.concatenate([gath[i * gxs + h, gx] for h in range(gxs)], axis=0) for i in range(3)]
    new = [jnp.concatenate([fresh[h, i, gx] for h in range(gxs)], axis=0) for i in range(3)]
    stacked = jnp.concatenate([jnp.concatenate(old, axis=1), jnp.concatenate(new, axis=1)], axis=0)
    picked = dot(stacked.astype(BF), pick)
    source = picked[:x_length].astype(BF)
    target = picked[x_length:]

    for b in range(pairs // 2):
        cols = slice(b * 256, (b + 1) * 256)
        lifted = dot(source, lift_big[:, cols]).astype(BF)
        lifted_ref[:, cols] = lifted
        coeffs = dot(table, lifted) * scale_dft
        stage[2 * b * 64 : (2 * b + 1) * 64, :] = coeffs[:, :128]
        stage[(2 * b + 1) * 64 : (2 * b + 2) * 64, :] = coeffs[:, 128:]

    def mode_rows(m, rows_of, keep):
        real = stage[pl.ds(m, rows_of, stride=64), :]
        imag = stage[pl.ds(modes + m, rows_of, stride=64), :]
        low = iota((rows_of, 128), 1) < 64
        top = jnp.where(low, real, pltpu.roll(imag, 64, 1))
        bottom = jnp.where(low, pltpu.roll(real, 64, 1), imag)
        keep(jnp.concatenate([top[:8], bottom[:8], top[8:], bottom[8:]][: rows_of // 4], axis=0))

    def all_modes(body):
        def step(m, carry):
            body(m)
            return carry

        lax.fori_loop(0, modes, step, 0, unroll=8)

    def exchange(src, dst, sems, place, sent):
        return pltpu.make_async_remote_copy(
            src_ref=src,
            dst_ref=dst,
            send_sem=sems.at[0, sent],
            recv_sem=sems.at[1, 0],
            device_id=place,
            device_id_type=MESH,
        )

    def keep_own(src, dst, sems):
        pltpu.make_async_copy(src, dst, sems.at[1, 0]).start()

    def await_all(buffer, sems):
        pltpu.make_async_copy(buffer, buffer, sems.at[1, 0]).wait()

    def a_copy(place, t, at):
        return exchange(a_own.at[t], a_all.at[at], a_sems, place, t)

    def d_copy(part, place, t, at):
        return exchange(d_own.at[part, t], d_all.at[part, at], d_sems[part], place, t)

    def m_copy(place, t, at):
        return exchange(m_part.at[t], m_recv.at[at], m_sems, place, t)

    def r_copy(place, t, at):
        return exchange(m_row, m_all.at[at], r_sems, place, t)

    def keep_a(m):
        def keep(rows):
            both = rows.astype(BF)
            a_own[m // gys, m % gys, 0] = both[:16]
            a_own[m // gys, m % gys, 1] = both[16:]

        mode_rows(m, pairs, keep)

    all_modes(keep_a)
    for place, t in near_peers:
        a_copy(place, t, slot).start()
    keep_own(a_own.at[slot], a_all.at[slot], a_sems)

    def mix_mode(m):
        out = dot(a_own[m // gys, m % gys].reshape(lines, 2 * chans), wide_mix[m])
        top = jnp.concatenate([out[:8], out[16:24]], axis=0)
        bottom = jnp.concatenate([out[8:16], out[24:]], axis=0)
        stage_out[pl.ds(m, pairs, stride=64), :] = jnp.where(
            low16, top, pltpu.roll(bottom, 64, 1)
        )
        stage_out[pl.ds(modes + m, pairs, stride=64), :] = jnp.where(
            low16, pltpu.roll(top, 64, 1), bottom
        )

    all_modes(mix_mode)

    root = math.sqrt(2.0 / math.pi)
    mix_sum = jnp.zeros((128, 128), F32)
    for half_lines in range(2):
        blocks = range(half_lines * 4, half_lines * 4 + 4)
        predicted = jnp.zeros((x_length, 128), F32)
        for b in blocks:
            cols = slice(b * 256, (b + 1) * 256)
            mixed = jnp.concatenate(
                [
                    stage_out[2 * b * 64 : (2 * b + 1) * 64, :],
                    stage_out[(2 * b + 1) * 64 : (2 * b + 2) * 64, :],
                ],
                axis=1,
            ).astype(BF)
            hidden = dot(table_t, mixed) * (2.0 * scale_dft) + dot(lifted_ref[:, cols], mix_four)
            squared = hidden * hidden
            bent = jnp.tanh(root * hidden * (1.0 + 0.044715 * squared))
            upper = 0.5 * (1.0 + bent)
            active = (hidden * upper).astype(BF)
            slope_ref[:, cols] = upper + 0.5 * hidden * (1.0 - bent * bent) * (
                root * (1.0 + 3.0 * 0.044715 * squared)
            )
            predicted = predicted + dot(active, proj_down[b * 256 : (b + 1) * 256, :])
        misfit = (predicted - target) * loss_scale
        coarse = misfit.astype(BF)
        fine = (misfit - coarse.astype(F32)).astype(BF)
        misfit_parts = jnp.concatenate([coarse, fine], axis=1)
        for b in blocks:
            cols = slice(b * 256, (b + 1) * 256)
            back_active = dot(misfit_parts, proj_up[:, cols])
            back_hidden = (slope_ref[:, cols] * back_active).astype(BF)
            lifted = lifted_ref[:, cols]
            for part in range(2):
                lanes = slice(part * 128, (part + 1) * 128)
                mix_sum = mix_sum + dot(lifted[:, lanes], back_hidden[:, lanes], ((0,), (0,)))
            back = dot(table, back_hidden) * (2.0 * scale_dft)
            at = 2 * (b % 4) * 64
            stage[at : at + 64, :] = back[:, :128]
            stage[at + 64 : at + 128, :] = back[:, 128:]

        if half_lines == 1:
            mix_own = mix_sum[:64] + pltpu.roll(mix_sum[64:], 64, 1)
            packed = jnp.where(
                iota((32, 128), 1) < 64, mix_own[:32], pltpu.roll(mix_own[32:], 64, 1)
            )
            for row in range(count):
                m_part[row] = packed[row : row + 1, :]
            for place, t in peers:
                m_copy(place, t, me).start()
            keep_own(m_part.at[me], m_recv.at[me], m_sems)

        def keep_d(m):
            def keep(rows):
                d_own[half_lines, m // gys, m % gys] = rows.astype(BF)

            mode_rows(m, pairs // 2, keep)

        all_modes(keep_d)
        for place, t in near_peers:
            d_copy(half_lines, place, t, slot).start()
        keep_own(d_own.at[half_lines, slot], d_all.at[half_lines, slot], d_sems[half_lines])

    await_all(m_recv, m_sems)
    total = jnp.sum(m_recv[...], axis=0)
    m_row[...] = total
    keep_own(m_row, m_all.at[me], r_sems)
    for place, t in peers:
        r_copy(place, t, me).start()

    await_all(a_all, a_sems)
    sums = [jnp.zeros((128, 128), F32) for _ in range(gys)]
    for half_lines in range(2):
        await_all(d_all.at[half_lines], d_sems[half_lines])
        for q in range(gys):
            a_lines = a_all[:, q, half_lines].reshape(near * 16, 2 * chans)
            d_lines = d_all[half_lines, :, q].reshape(near * 16, 2 * chans)
            sums[q] = sums[q] + dot(a_lines, d_lines, ((0,), (0,)))
    for q in range(gys):
        turned_sum = pltpu.roll(sums[q][64:], 64, 1)
        g_part[q] = sums[q][:64] + jnp.where(low_half, turned_sum, -turned_sum)

    def g_copy(d):
        place = {"grp": g, "gx": gx, "gy": y_at[d]}
        return exchange(g_part.at[y_at[d]], g_recv.at[gy], g_sems, place, d)

    for d in range(1, gys):
        g_copy(d).start()
    keep_own(g_part.at[gy], g_recv.at[gy], g_sems)
    await_all(g_recv, g_sems)
    grad_ref[...] = jnp.sum(g_recv[...], axis=0)

    await_all(m_all, r_sems)
    rows = jnp.concatenate([m_all[row] for row in range(count)], axis=0)
    mixg_ref[...] = jnp.concatenate([rows[:, :64], rows[:, 64:]], axis=0)

    result_copy.wait()
    for place, s in near_peers:
        field_copy(place, s, slot).wait_send()
        a_copy(place, s, slot).wait_send()
        d_copy(0, place, s, slot).wait_send()
        d_copy(1, place, s, slot).wait_send()
    for d in range(1, gys):
        g_copy(d).wait_send()
    solid_copy.wait_send()

    @pl.when(gy > 0)
    def _():
        each_near(lambda s: rim_copy(0, s, slot).wait_send())

    @pl.when(gy < gys - 1)
    def _():
        each_near(lambda s: rim_copy(1, s, slot).wait_send())

    for place, t in peers:
        m_copy(place, t, me).wait_send()
        r_copy(place, t, me).wait_send()


def fused(sizes, slot_field, solid, lift_weight, spectral_weight, mix_weight, project_weight, mode_index):
    grps, gxs, gys, x_length, _ = sizes
    count = grps * gxs * gys
    near = grps * gxs
    half = x_length // gxs
    dma = pltpu.SemaphoreType.DMA
    vmem = pl.BlockSpec(memory_space=pltpu.VMEM)
    whole = pl.BlockSpec(memory_space=pl.ANY)
    shape = jax.ShapeDtypeStruct
    return pl.pallas_call(
        functools.partial(fused_kernel, sizes),
        out_shape=(
            shape((3, 2, half, 128), F32),
            shape((64, 128), F32),
            shape((64, 64), F32),
        ),
        in_specs=[whole, whole, vmem, whole, vmem, vmem, vmem],
        out_specs=(whole, vmem, vmem),
        scratch_shapes=[
            pltpu.VMEM((64 * count, 128), BF),
            pltpu.VMEM((near, 2, half, 128), F32),
            pltpu.VMEM((gxs, 2, half, 128), jnp.int32),
            pltpu.VMEM((2, 1, 128), F32),
            pltpu.VMEM((2, near, 1, 128), F32),
            pltpu.VMEM((gxs, 3, 2, half, 128), F32),
            pltpu.VMEM((count, 128, 128), BF),
            pltpu.VMEM((128, 2048), BF),
            pltpu.VMEM((2048, 128), BF),
            pltpu.VMEM((256, 2048), BF),
            pltpu.VMEM((x_length, 2048), BF),
            pltpu.VMEM((x_length, 2048), F32),
            pltpu.VMEM((1024, 128), F32),
            pltpu.VMEM((1024, 128), F32),
            pltpu.VMEM((near, gys, 2, 16, 128), BF),
            pltpu.VMEM((2, near, gys, 16, 128), BF),
            pltpu.VMEM((near, gys, 2, 16, 128), BF),
            pltpu.VMEM((2, near, gys, 16, 128), BF),
            pltpu.VMEM((count, 1, 128), F32),
            pltpu.VMEM((count, 1, 128), F32),
            pltpu.VMEM((1, 128), F32),
            pltpu.VMEM((count, 1, 128), F32),
            pltpu.VMEM((gys, 64, 128), F32),
            pltpu.VMEM((gys, 64, 128), F32),
            dma((4,)),
            dma((near,)),
            dma((near,)),
            dma((2,)),
            dma((2, near)),
            dma((2, near)),
        ]
        + [dma((2, count))] * 6,
        compiler_params=pltpu.CompilerParams(
            collective_id=0, has_side_effects=True, vmem_limit_bytes=60 * 1024 * 1024
        ),
        cost_estimate=pl.CostEstimate(
            flops=400_000_000, bytes_accessed=2_000_000, transcendentals=200_000
        ),
    )(
        slot_field,
        solid,
        lift_weight,
        spectral_weight,
        mix_weight,
        jnp.transpose(project_weight),
        mode_index.reshape(1, -1),
    )


def local(slot_field, solid, lift_weight, spectral_weight, mix_weight, project_weight, mode_index):
    arrays = (slot_field, solid, lift_weight, spectral_weight, mix_weight, project_weight, mode_index)
    grps, gxs, gys = (lax.axis_size(axis) for axis in ("grp", "gx", "gy"))
    _, planes, x_rows, y_cols = slot_field.shape
    x_length = x_rows * gxs
    sizes = (grps, gxs, gys, x_length, x_length * y_cols * gys * planes)
    fits = (
        grps * gxs * gys == mode_index.shape[0] == 32
        and mix_weight.shape[0] == 64
        and gxs == planes == 2
        and y_cols == 32 * grps == 128
        and x_rows == 48
    )
    if fits:
        return fused(sizes, *arrays)
    return general(*arrays)


def solution(mesh):
    in_specs = (P("grp", None, "gx", "gy"), P(None, "gx", "gy"), P(), P(), P(), P(), P())
    out_specs = (P(None, None, "gx", "gy"), P(("grp", "gx", "gy"), None), P())
    return jax.shard_map(local, mesh=mesh, in_specs=in_specs, out_specs=out_specs, check_vma=False)
```

```python
import functools
import math

import jax
import jax.numpy as jnp
from jax import lax
from jax.experimental import pallas as pl
from jax.experimental.pallas import tpu as pltpu
from jax.sharding import PartitionSpec as P

VISCOSITY = 0.05
TIME_STEP = 0.1


def with_halo(block, sides, width):
    for axis, dim in sides:
        count = lax.axis_size(axis)
        forward = [(i, i + 1) for i in range(count - 1)]
        backward = [(target, source) for source, target in forward]
        low = lax.ppermute(
            lax.slice_in_dim(block, block.shape[dim] - width, None, axis=dim), axis, forward
        )
        high = lax.ppermute(lax.slice_in_dim(block, 0, width, axis=dim), axis, backward)
        block = jnp.concatenate([low, block, high], axis=dim)
    return block


def interior(source):
    return source[1:-1, 1:-1, 1:-1]


def along_x(source):
    return 0.5 * (source[1:-1, 2:, 1:-1] - source[1:-1, :-2, 1:-1])


def along_y(source):
    return 0.5 * (source[1:-1, 1:-1, 2:] - source[1:-1, 1:-1, :-2])


def along_z(source):
    return 0.5 * (source[2:, 1:-1, 1:-1] - source[:-2, 1:-1, 1:-1])


def laplace(source):
    total = source[2:, 1:-1, 1:-1] + source[:-2, 1:-1, 1:-1]
    total = total + source[1:-1, 2:, 1:-1] + source[1:-1, :-2, 1:-1]
    total = total + source[1:-1, 1:-1, 2:] + source[1:-1, 1:-1, :-2]
    return total - 6.0 * interior(source)


def section_component(padded, component, solid):
    source = padded[component]
    velocity = [interior(padded[index]) for index in range(3)]
    advect = (
        velocity[0] * along_x(source)
        + velocity[1] * along_y(source)
        + velocity[2] * along_z(source)
    )
    pressure = padded[3]
    press_grad = jnp.stack([along_x(pressure), along_y(pressure), along_z(pressure)])[component]
    update = interior(source) + TIME_STEP * (VISCOSITY * laplace(source) - advect - press_grad)
    return update * (1.0 - solid.astype(jnp.float32))


def spectral_table(mode_index, x_length):
    places = jnp.arange(x_length, dtype=jnp.int32)
    phases = mode_index[:, None] * places[None, :] % x_length
    angles = 2.0 * jnp.pi / x_length * phases.astype(jnp.float32)
    return jnp.concatenate([jnp.cos(angles), -jnp.sin(angles)], axis=0).astype(jnp.bfloat16)


def contract(form, left, right):
    return jnp.einsum(form, left, right, preferred_element_type=jnp.float32)


def student_terms(
    line_data,
    dft_table,
    lift_weight,
    spectral_weight,
    mix_weight,
    project_weight,
    loss_scale,
    x_length,
):
    mode_count = dft_table.shape[0] // 2
    chan_count = mix_weight.shape[0]
    scale_dft = 1.0 / math.sqrt(x_length)
    old_part = line_data[:3]
    target = line_data[3:].astype(jnp.float32)
    lifted = contract("iln,ic->cln", old_part, lift_weight).astype(jnp.bfloat16)
    coeffs = (contract("cln,mn->clm", lifted, dft_table) * scale_dft).astype(jnp.bfloat16)
    real_in = coeffs[..., :mode_count]
    imag_in = coeffs[..., mode_count:]
    weights = spectral_weight.reshape(mode_count, chan_count, 2 * chan_count)
    real_w = weights[..., :chan_count]
    imag_w = weights[..., chan_count:]
    real_out = contract("clm,mco->olm", real_in, real_w) - contract("clm,mco->olm", imag_in, imag_w)
    imag_out = contract("clm,mco->olm", real_in, imag_w) + contract("clm,mco->olm", imag_in, real_w)
    mixed = jnp.concatenate([real_out, imag_out], axis=2).astype(jnp.bfloat16)
    spectral = contract("olm,mn->oln", mixed, dft_table) * (2.0 * scale_dft)
    local_term = contract("cln,co->oln", lifted, mix_weight)
    hidden = spectral + local_term
    active, gelu_back = jax.vjp(jax.nn.gelu, hidden)
    active = active.astype(jnp.bfloat16)
    predicted = contract("oln,oi->iln", active, project_weight)
    misfit = (predicted - target) * loss_scale
    back_active = jnp.einsum(
        "iln,oi->oln", misfit, project_weight.astype(jnp.float32), precision=lax.Precision.HIGHEST
    )
    back_hidden = gelu_back(back_active)[0].astype(jnp.bfloat16)
    mix_part = contract("cln,oln->co", lifted, back_hidden)
    back_mixed = (contract("oln,mn->olm", back_hidden, dft_table) * (2.0 * scale_dft)).astype(
        jnp.bfloat16
    )
    back_real = back_mixed[..., :mode_count]
    back_imag = back_mixed[..., mode_count:]
    grad_real = contract("clm,olm->mco", real_in, back_real) + contract(
        "clm,olm->mco", imag_in, back_imag
    )
    grad_imag = contract("clm,olm->mco", real_in, back_imag) - contract(
        "clm,olm->mco", imag_in, back_real
    )
    spectral_part = jnp.concatenate([grad_real, grad_imag], axis=2).reshape(
        mode_count * chan_count, 2 * chan_count
    )
    return (spectral_part, mix_part)


def general(slot_field, solid, lift_weight, spectral_weight, mix_weight, project_weight, mode_index):
    role_index = lax.axis_index("grp")
    own_tile = slot_field[0]
    planes, x_rows, y_cols = own_tile.shape
    x_length = x_rows * lax.axis_size("gx")
    cell_total = x_length * y_cols * lax.axis_size("gy") * planes
    loss_scale = 16.0 / math.sqrt(cell_total)
    dft_table = spectral_table(mode_index, x_length)
    rimmed = with_halo(own_tile, (("gx", 1), ("gy", 2)), 1)
    gathered = lax.all_gather(rimmed[None], "grp", axis=0, tiled=True)
    padded = jnp.pad(gathered, ((0, 0), (1, 1), (0, 0), (0, 0)))
    old_velocity = gathered[:3, :, 1:-1, 1:-1]
    new_tile = lax.cond(
        role_index < 3,
        lambda: section_component(padded, jnp.minimum(role_index, 2), solid),
        lambda: own_tile,
    )
    new_slots = lax.all_gather(new_tile[None], "grp", axis=0, tiled=True)
    new_velocity = new_slots[:3]
    both_fields = jnp.concatenate([old_velocity, new_velocity], axis=0).astype(jnp.bfloat16)
    pencil_data = lax.all_to_all(
        jnp.transpose(both_fields, (0, 1, 3, 2)), "gx", split_axis=2, concat_axis=3, tiled=True
    )
    line_data = pencil_data.reshape(6, -1, x_length)

    def student(own_lines):
        return student_terms(
            own_lines,
            dft_table,
            lift_weight,
            spectral_weight,
            mix_weight,
            project_weight,
            loss_scale,
            x_length,
        )

    def nothing():
        return (
            jnp.zeros(spectral_weight.shape, jnp.float32),
            jnp.zeros(mix_weight.shape, jnp.float32),
        )

    spectral_part, mix_part = lax.cond(role_index == 3, lambda: student(line_data), nothing)
    spectral_grad = lax.psum_scatter(
        spectral_part, ("grp", "gx", "gy"), scatter_dimension=0, tiled=True
    )
    mix_grad = lax.psum(mix_part, ("grp", "gx", "gy"))
    return (new_velocity, spectral_grad, mix_grad)


MESH = pl.DeviceIdType.MESH
BF = jnp.bfloat16
F32 = jnp.float32


def dot(left, right, contract_dims=((1,), (0,))):
    return lax.dot_general(left, right, (contract_dims, ((), ())), preferred_element_type=F32)


def iota(shape, dim):
    return lax.broadcasted_iota(jnp.int32, shape, dim)


def fused_kernel(
    sizes,
    field_ref,
    solid_ref,
    lift_ref,
    spec_ref,
    mix_ref,
    proj_ref,
    mode_ref,
    newv_ref,
    grad_ref,
    mixg_ref,
    spec_vm,
    gath,
    both_solid,
    edge,
    rims,
    fresh,
    wide_mix,
    lift_big,
    proj_down,
    proj_up,
    lifted_ref,
    slope_ref,
    stage,
    stage_out,
    a_own,
    d_own,
    a_all,
    d_all,
    m_part,
    m_recv,
    m_row,
    m_all,
    m_plane,
    m_planes,
    g_part,
    g_recv,
    load,
    field_send,
    field_recv,
    solid_sem,
    rim_send,
    rim_recv,
    a_sems,
    d_sems_a,
    d_sems_b,
    m_sems,
    r_sems,
    g_sems,
    z_sems,
):
    grps, gxs, gys, x_length, cell_total = sizes
    count = grps * gxs * gys
    near = grps * gxs
    half = x_length // gxs
    modes = count
    lines = 32
    pairs = lines // 2
    chans = 64
    g = lax.axis_index("grp")
    gx = lax.axis_index("gx")
    gy = lax.axis_index("gy")
    me = (g * gxs + gx) * gys + gy
    slot = g * gxs + gx
    scale_dft = 1.0 / math.sqrt(x_length)
    loss_scale = 16.0 / math.sqrt(cell_total)
    d_sems = (d_sems_a, d_sems_b)

    g_at = [(g + d) % grps for d in range(grps)]
    x_at = [(gx + d) % gxs for d in range(gxs)]
    y_at = [(gy + d) % gys for d in range(gys)]
    peers = []
    for dy in [gys // 2] + [d for d in range(gys) if d != gys // 2]:
        for dg in range(grps):
            for dx in range(gxs):
                if (dg, dx, dy) != (0, 0, 0):
                    place = {"grp": g_at[dg], "gx": x_at[dx], "gy": y_at[dy]}
                    peers.append((place, (g_at[dg] * gxs + x_at[dx]) * gys + y_at[dy]))

    barrier = pltpu.get_barrier_semaphore()
    for place, _ in peers:
        pl.semaphore_signal(barrier, inc=1, device_id=place, device_id_type=MESH)

    loads = [
        pltpu.make_async_copy(field_ref.at[0], gath.at[slot], load.at[0]),
        pltpu.make_async_copy(solid_ref, both_solid.at[gx], load.at[1]),
        pltpu.make_async_copy(spec_ref, spec_vm, load.at[2]),
    ]
    for copy in loads:
        copy.start()
    loads[0].wait()

    own = gath[pl.ds(slot, 1)][0]
    flat = jnp.concatenate([own.reshape(2 * half, 128), jnp.zeros((128 - 2 * half, 128), F32)], axis=0)
    turned = jnp.transpose(flat)
    edge[0] = turned[0:1, :]
    edge[1] = turned[127:128, :]

    @pl.when(gy == 0)
    def _():
        rims[0] = jnp.zeros((near, 1, 128), F32)

    @pl.when(gy == gys - 1)
    def _():
        rims[1] = jnp.zeros((near, 1, 128), F32)

    pl.semaphore_wait(barrier, count - 1)

    near_peers = []
    for dg in range(grps):
        for dx in range(gxs):
            if (dg, dx) != (0, 0):
                place = {"grp": g_at[dg], "gx": x_at[dx], "gy": gy}
                near_peers.append((place, g_at[dg] * gxs + x_at[dx]))

    def field_copy(place, s, at):
        return pltpu.make_async_remote_copy(
            src_ref=field_ref.at[0],
            dst_ref=gath.at[at],
            send_sem=field_send.at[s],
            recv_sem=field_recv.at[at],
            device_id=place,
            device_id_type=MESH,
        )

    def rim_copy(side, s, at):
        return pltpu.make_async_remote_copy(
            src_ref=edge.at[side],
            dst_ref=rims.at[1 - side, at],
            send_sem=rim_send.at[side, s],
            recv_sem=rim_recv.at[1 - side, at],
            device_id={"grp": s // gxs, "gx": s % gxs, "gy": gy - 1 + 2 * side},
            device_id_type=MESH,
        )

    def each_near(body):
        def step(s, carry):
            body(s)
            return carry

        lax.fori_loop(0, near, step, 0)

    for place, s in near_peers:
        field_copy(place, s, slot).start()

    @pl.when(gy > 0)
    def _():
        each_near(lambda s: rim_copy(0, s, slot).start())

    @pl.when(gy < gys - 1)
    def _():
        each_near(lambda s: rim_copy(1, s, slot).start())

    solid_copy = pltpu.make_async_remote_copy(
        src_ref=solid_ref,
        dst_ref=both_solid.at[gx],
        send_sem=solid_sem.at[0],
        recv_sem=solid_sem.at[1],
        device_id={"grp": g, "gx": x_at[1], "gy": gy},
        device_id_type=MESH,
    )
    solid_copy.start()
    for copy in loads[1:]:
        copy.wait()

    lane = iota((x_length, 128), 1)
    low16 = iota((16, 128), 1) < 64
    mode_row = mode_ref[...].astype(F32)
    mode_row = jnp.concatenate([mode_row] * 4, axis=1)
    place = iota((x_length, 128), 0).astype(F32)
    raw = mode_row * place + jnp.where(lane >= modes, 0.25 * x_length, 0.0)
    phase = raw - x_length * jnp.floor((raw + 0.5) * (1.0 / x_length))
    phase = jnp.where(phase >= 0.5 * x_length, phase - x_length, phase)
    angle = phase * (math.pi / x_length)
    square = angle * angle
    series = jnp.full_like(square, -1.0 / 39916800.0)
    for term in (1.0 / 362880.0, -1.0 / 5040.0, 1.0 / 120.0, -1.0 / 6.0, 1.0):
        series = series * square + term
    sine = series * angle
    waves = 1.0 - 2.0 * sine * sine
    table_t = waves[:, : 2 * modes].astype(BF)
    table = jnp.transpose(jnp.concatenate([waves, jnp.zeros((128 - x_length, 128), F32)], axis=0))
    table = table[: 2 * modes, :x_length].astype(BF)

    row128 = iota((128, 128), 0)
    col128 = iota((128, 128), 1)
    lift = lift_ref[...].astype(F32)
    lift = jnp.concatenate([lift, lift], axis=1)
    lift_rows = jnp.where(
        row128 < 32,
        lift[0:1],
        jnp.where(row128 < 64, lift[1:2], jnp.where(row128 < 96, lift[2:3], 0.0)),
    )
    proj = proj_ref[...].astype(F32)
    proj = jnp.concatenate([proj, proj], axis=1)
    proj_rows = jnp.where(
        row128 < 32,
        proj[0:1],
        jnp.where(row128 < 64, proj[1:2], jnp.where(row128 < 96, proj[2:3], 0.0)),
    )
    proj_cols = jnp.transpose(proj_rows)[:64]
    col64 = iota((64, 128), 1)
    line_of_row = jnp.bitwise_and(row128, 31)
    half_of_lane = jnp.where(col128 < 64, 0, 1)
    line_of_col = jnp.bitwise_and(col64, 31)

    def widen(p, carry):
        hit = line_of_row == 2 * p + half_of_lane
        cols = pl.ds(pl.multiple_of(p * 128, 128), 128)
        lift_big[:, cols] = jnp.where(hit, lift_rows, 0.0).astype(BF)
        up = jnp.where(hit, proj_rows, 0.0).astype(BF)
        proj_up[0:128, cols] = up
        proj_up[128:256, cols] = up
        for part in range(2):
            down = jnp.where(line_of_col == 2 * p + part, proj_cols, 0.0).astype(BF)
            proj_down[pl.ds(pl.multiple_of(p * 128 + part * 64, 64), 64), :] = down
        return carry

    lax.fori_loop(0, pairs, widen, 0)

    low_half = col64 < 64

    def widen_mix(m, carry):
        block = spec_vm[pl.ds(pl.multiple_of(m * 64, 64), 64), :]
        wide = block.astype(F32)
        turned_block = pltpu.roll(wide, 64, 1)
        wide_mix[m, 0:64, :] = block
        wide_mix[m, 64:128, :] = jnp.where(low_half, -turned_block, turned_block).astype(BF)
        return carry

    lax.fori_loop(0, modes, widen_mix, 0)

    mix = mix_ref[...].astype(F32)
    mix = jnp.concatenate([mix, mix], axis=1)
    mix = jnp.concatenate([mix, mix], axis=0)
    mix = jnp.where((row128 < 64) == (col128 < 64), mix, 0.0)
    blank = jnp.zeros_like(mix)
    mix_four = jnp.concatenate(
        [jnp.concatenate([mix, blank], axis=1), jnp.concatenate([blank, mix], axis=1)], axis=0
    ).astype(BF)
    pick = jnp.concatenate(
        [
            jnp.where((col128 // 32 == i) & (row128 == 32 * g + jnp.bitwise_and(col128, 31)), 1.0, 0.0)
            for i in range(3)
        ],
        axis=0,
    ).astype(BF)

    for place, s in near_peers:
        field_copy(place, s, s).wait_recv()
    solid_copy.wait_recv()

    @pl.when(gy > 0)
    def _():
        each_near(lambda s: rim_copy(1, s, s).wait_recv())

    @pl.when(gy < gys - 1)
    def _():
        each_near(lambda s: rim_copy(0, s, s).wait_recv())

    rim_rows = [rims[side, s] for side in range(2) for s in range(near)]
    rim_rows.append(jnp.zeros((128 - 2 * near, 128), F32))
    rim_cols = jnp.transpose(jnp.concatenate(rim_rows, axis=0))
    first_row = iota((x_length, 128), 0) == 0
    last_row = iota((x_length, 128), 0) == x_length - 1

    def whole(f, z):
        return jnp.concatenate([gath[f * gxs + h, z] for h in range(gxs)], axis=0)

    def rim(f, z, side):
        cols = [
            rim_cols[z * half : (z + 1) * half, side * near + f * gxs + h :][:, 0:1] for h in range(gxs)
        ]
        return jnp.concatenate(cols, axis=0)

    def shifted(f, z, value):
        x_up = jnp.where(last_row, 0.0, pltpu.roll(value, x_length - 1, 0))
        x_down = jnp.where(first_row, 0.0, pltpu.roll(value, 1, 0))
        y_up = jnp.where(lane == 127, rim(f, z, 1), pltpu.roll(value, 127, 1))
        y_down = jnp.where(lane == 0, rim(f, z, 0), pltpu.roll(value, 1, 1))
        return x_up, x_down, y_up, y_down

    for z in range(2):
        fluid = 1.0 - jnp.concatenate([both_solid[h, z] for h in range(gxs)], axis=0).astype(F32)
        here = [whole(f, z) for f in range(4)]
        there = [whole(f, 1 - z) for f in range(4)]
        sign_z = 0.5 if z == 0 else -0.5
        press = shifted(3, z, here[3])
        grads = (0.5 * (press[0] - press[1]), 0.5 * (press[2] - press[3]), sign_z * there[3])
        for k in range(3):
            x_up, x_down, y_up, y_down = shifted(k, z, here[k])
            lap = there[k] + x_up + x_down + y_up + y_down - 6.0 * here[k]
            advect = (
                here[0] * (0.5 * (x_up - x_down))
                + here[1] * (0.5 * (y_up - y_down))
                + here[2] * (sign_z * there[k])
            )
            update = here[k] + TIME_STEP * (VISCOSITY * lap - advect - grads[k])
            update = update * fluid
            for h in range(gxs):
                fresh[h, k, z] = update[h * half : (h + 1) * half]
    result_copy = pltpu.make_async_copy(fresh.at[gx], newv_ref, load.at[3])
    result_copy.start()

    old = [jnp.concatenate([gath[i * gxs + h, gx] for h in range(gxs)], axis=0) for i in range(3)]
    new = [jnp.concatenate([fresh[h, i, gx] for h in range(gxs)], axis=0) for i in range(3)]
    stacked = jnp.concatenate([jnp.concatenate(old, axis=1), jnp.concatenate(new, axis=1)], axis=0)
    picked = dot(stacked.astype(BF), pick)
    source = picked[:x_length].astype(BF)
    target = picked[x_length:]

    for b in range(pairs // 2):
        cols = slice(b * 256, (b + 1) * 256)
        lifted = dot(source, lift_big[:, cols]).astype(BF)
        lifted_ref[:, cols] = lifted
        coeffs = dot(table, lifted) * scale_dft
        stage[2 * b * 64 : (2 * b + 1) * 64, :] = coeffs[:, :128]
        stage[(2 * b + 1) * 64 : (2 * b + 2) * 64, :] = coeffs[:, 128:]

    def mode_rows(m, rows_of, keep):
        real = stage[pl.ds(m, rows_of, stride=64), :]
        imag = stage[pl.ds(modes + m, rows_of, stride=64), :]
        low = iota((rows_of, 128), 1) < 64
        top = jnp.where(low, real, pltpu.roll(imag, 64, 1))
        bottom = jnp.where(low, pltpu.roll(real, 64, 1), imag)
        keep(jnp.concatenate([top[:8], bottom[:8], top[8:], bottom[8:]][: rows_of // 4], axis=0))

    def all_modes(body):
        def step(m, carry):
            body(m)
            return carry

        lax.fori_loop(0, modes, step, 0, unroll=8)

    def exchange(src, dst, sems, place, sent):
        return pltpu.make_async_remote_copy(
            src_ref=src,
            dst_ref=dst,
            send_sem=sems.at[0, sent],
            recv_sem=sems.at[1, 0],
            device_id=place,
            device_id_type=MESH,
        )

    def keep_own(src, dst, sems):
        pltpu.make_async_copy(src, dst, sems.at[1, 0]).start()

    def await_all(buffer, sems):
        pltpu.make_async_copy(buffer, buffer, sems.at[1, 0]).wait()

    def a_copy(place, t, at):
        return exchange(a_own.at[t], a_all.at[at], a_sems, place, t)

    def d_copy(part, place, t, at):
        return exchange(d_own.at[part, t], d_all.at[part, at], d_sems[part], place, t)

    def m_copy(place, t, at):
        return exchange(m_part.at[t], m_recv.at[at], m_sems, place, t)

    def r_copy(place, t, at):
        return exchange(m_row, m_all.at[at], r_sems, place, t)

    def keep_a(m):
        def keep(rows):
            both = rows.astype(BF)
            a_own[m // gys, m % gys, 0] = both[:16]
            a_own[m // gys, m % gys, 1] = both[16:]

        mode_rows(m, pairs, keep)

    all_modes(keep_a)
    for place, t in near_peers:
        a_copy(place, t, slot).start()
    keep_own(a_own.at[slot], a_all.at[slot], a_sems)

    def mix_mode(m):
        out = dot(a_own[m // gys, m % gys].reshape(lines, 2 * chans), wide_mix[m])
        top = jnp.concatenate([out[:8], out[16:24]], axis=0)
        bottom = jnp.concatenate([out[8:16], out[24:]], axis=0)
        stage_out[pl.ds(m, pairs, stride=64), :] = jnp.where(
            low16, top, pltpu.roll(bottom, 64, 1)
        )
        stage_out[pl.ds(modes + m, pairs, stride=64), :] = jnp.where(
            low16, pltpu.roll(top, 64, 1), bottom
        )

    all_modes(mix_mode)

    root = math.sqrt(2.0 / math.pi)
    mix_sum = jnp.zeros((128, 128), F32)
    for half_lines in range(2):
        blocks = range(half_lines * 4, half_lines * 4 + 4)
        predicted = jnp.zeros((x_length, 128), F32)
        for b in blocks:
            cols = slice(b * 256, (b + 1) * 256)
            mixed = jnp.concatenate(
                [
                    stage_out[2 * b * 64 : (2 * b + 1) * 64, :],
                    stage_out[(2 * b + 1) * 64 : (2 * b + 2) * 64, :],
                ],
                axis=1,
            ).astype(BF)
            hidden = dot(table_t, mixed) * (2.0 * scale_dft) + dot(lifted_ref[:, cols], mix_four)
            squared = hidden * hidden
            bent = jnp.tanh(root * hidden * (1.0 + 0.044715 * squared))
            upper = 0.5 * (1.0 + bent)
            active = (hidden * upper).astype(BF)
            slope_ref[:, cols] = upper + 0.5 * hidden * (1.0 - bent * bent) * (
                root * (1.0 + 3.0 * 0.044715 * squared)
            )
            predicted = predicted + dot(active, proj_down[b * 256 : (b + 1) * 256, :])
        misfit = (predicted - target) * loss_scale
        coarse = misfit.astype(BF)
        fine = (misfit - coarse.astype(F32)).astype(BF)
        misfit_parts = jnp.concatenate([coarse, fine], axis=1)
        for b in blocks:
            cols = slice(b * 256, (b + 1) * 256)
            back_active = dot(misfit_parts, proj_up[:, cols])
            back_hidden = (slope_ref[:, cols] * back_active).astype(BF)
            lifted = lifted_ref[:, cols]
            for part in range(2):
                lanes = slice(part * 128, (part + 1) * 128)
                mix_sum = mix_sum + dot(lifted[:, lanes], back_hidden[:, lanes], ((0,), (0,)))
            back = dot(table, back_hidden) * (2.0 * scale_dft)
            at = 2 * (b % 4) * 64
            stage[at : at + 64, :] = back[:, :128]
            stage[at + 64 : at + 128, :] = back[:, 128:]

        if half_lines == 1:
            mix_own = mix_sum[:64] + pltpu.roll(mix_sum[64:], 64, 1)
            packed = jnp.where(
                iota((32, 128), 1) < 64, mix_own[:32], pltpu.roll(mix_own[32:], 64, 1)
            )
            for row in range(count):
                m_part[row // gys, row % gys] = packed[row : row + 1, :]
            for place, t in near_peers:
                m_copy(place, t, slot).start()
            keep_own(m_part.at[slot], m_recv.at[slot], m_sems)

        def keep_d(m):
            def keep(rows):
                d_own[half_lines, m // gys, m % gys] = rows.astype(BF)

            mode_rows(m, pairs // 2, keep)

        all_modes(keep_d)
        for place, t in near_peers:
            d_copy(half_lines, place, t, slot).start()
        keep_own(d_own.at[half_lines, slot], d_all.at[half_lines, slot], d_sems[half_lines])

    await_all(m_recv, m_sems)
    m_plane[...] = jnp.sum(m_recv[...], axis=0)

    def mz_copy(d):
        place = {"grp": g, "gx": gx, "gy": y_at[d]}
        return exchange(m_plane, m_planes.at[gy], z_sems, place, d)

    for d in range(1, gys):
        mz_copy(d).start()
    keep_own(m_plane, m_planes.at[gy], z_sems)

    await_all(a_all, a_sems)
    sums = [jnp.zeros((128, 128), F32) for _ in range(gys)]
    for half_lines in range(2):
        await_all(d_all.at[half_lines], d_sems[half_lines])
        for q in range(gys):
            a_lines = a_all[:, q, half_lines].reshape(near * 16, 2 * chans)
            d_lines = d_all[half_lines, :, q].reshape(near * 16, 2 * chans)
            sums[q] = sums[q] + dot(a_lines, d_lines, ((0,), (0,)))
    for q in range(gys):
        turned_sum = pltpu.roll(sums[q][64:], 64, 1)
        g_part[q] = sums[q][:64] + jnp.where(low_half, turned_sum, -turned_sum)

    def g_copy(d):
        place = {"grp": g, "gx": gx, "gy": y_at[d]}
        return exchange(g_part.at[y_at[d]], g_recv.at[gy], g_sems, place, d)

    for d in range(1, gys):
        g_copy(d).start()
    keep_own(g_part.at[gy], g_recv.at[gy], g_sems)
    await_all(m_planes, z_sems)
    m_row[...] = jnp.sum(m_planes[...], axis=0)
    for place, t in near_peers:
        r_copy(place, t, slot).start()
    keep_own(m_row, m_all.at[slot], r_sems)
    await_all(g_recv, g_sems)
    grad_ref[...] = jnp.sum(g_recv[...], axis=0)

    await_all(m_all, r_sems)
    rows = jnp.concatenate([m_all[row // gys, row % gys] for row in range(count)], axis=0)
    mixg_ref[...] = jnp.concatenate([rows[:, :64], rows[:, 64:]], axis=0)

    result_copy.wait()
    for place, s in near_peers:
        field_copy(place, s, slot).wait_send()
        a_copy(place, s, slot).wait_send()
        d_copy(0, place, s, slot).wait_send()
        d_copy(1, place, s, slot).wait_send()
        m_copy(place, s, slot).wait_send()
        r_copy(place, s, slot).wait_send()
    for d in range(1, gys):
        g_copy(d).wait_send()
        mz_copy(d).wait_send()
    solid_copy.wait_send()

    @pl.when(gy > 0)
    def _():
        each_near(lambda s: rim_copy(0, s, slot).wait_send())

    @pl.when(gy < gys - 1)
    def _():
        each_near(lambda s: rim_copy(1, s, slot).wait_send())


def fused(sizes, slot_field, solid, lift_weight, spectral_weight, mix_weight, project_weight, mode_index):
    grps, gxs, gys, x_length, _ = sizes
    count = grps * gxs * gys
    near = grps * gxs
    half = x_length // gxs
    dma = pltpu.SemaphoreType.DMA
    vmem = pl.BlockSpec(memory_space=pltpu.VMEM)
    whole = pl.BlockSpec(memory_space=pl.ANY)
    shape = jax.ShapeDtypeStruct
    return pl.pallas_call(
        functools.partial(fused_kernel, sizes),
        out_shape=(
            shape((3, 2, half, 128), F32),
            shape((64, 128), F32),
            shape((64, 64), F32),
        ),
        in_specs=[whole, whole, vmem, whole, vmem, vmem, vmem],
        out_specs=(whole, vmem, vmem),
        scratch_shapes=[
            pltpu.VMEM((64 * count, 128), BF),
            pltpu.VMEM((near, 2, half, 128), F32),
            pltpu.VMEM((gxs, 2, half, 128), jnp.int32),
            pltpu.VMEM((2, 1, 128), F32),
            pltpu.VMEM((2, near, 1, 128), F32),
            pltpu.VMEM((gxs, 3, 2, half, 128), F32),
            pltpu.VMEM((count, 128, 128), BF),
            pltpu.VMEM((128, 2048), BF),
            pltpu.VMEM((2048, 128), BF),
            pltpu.VMEM((256, 2048), BF),
            pltpu.VMEM((x_length, 2048), BF),
            pltpu.VMEM((x_length, 2048), F32),
            pltpu.VMEM((1024, 128), F32),
            pltpu.VMEM((1024, 128), F32),
            pltpu.VMEM((near, gys, 2, 16, 128), BF),
            pltpu.VMEM((2, near, gys, 16, 128), BF),
            pltpu.VMEM((near, gys, 2, 16, 128), BF),
            pltpu.VMEM((2, near, gys, 16, 128), BF),
            pltpu.VMEM((near, gys, 1, 128), F32),
            pltpu.VMEM((near, gys, 1, 128), F32),
            pltpu.VMEM((gys, 1, 128), F32),
            pltpu.VMEM((near, gys, 1, 128), F32),
            pltpu.VMEM((gys, 1, 128), F32),
            pltpu.VMEM((gys, gys, 1, 128), F32),
            pltpu.VMEM((gys, 64, 128), F32),
            pltpu.VMEM((gys, 64, 128), F32),
            dma((4,)),
            dma((near,)),
            dma((near,)),
            dma((2,)),
            dma((2, near)),
            dma((2, near)),
        ]
        + [dma((2, count))] * 7,
        compiler_params=pltpu.CompilerParams(
            collective_id=0, has_side_effects=True, vmem_limit_bytes=60 * 1024 * 1024
        ),
        cost_estimate=pl.CostEstimate(
            flops=400_000_000, bytes_accessed=2_000_000, transcendentals=200_000
        ),
    )(
        slot_field,
        solid,
        lift_weight,
        spectral_weight,
        mix_weight,
        jnp.transpose(project_weight),
        mode_index.reshape(1, -1),
    )


def local(slot_field, solid, lift_weight, spectral_weight, mix_weight, project_weight, mode_index):
    arrays = (slot_field, solid, lift_weight, spectral_weight, mix_weight, project_weight, mode_index)
    grps, gxs, gys = (lax.axis_size(axis) for axis in ("grp", "gx", "gy"))
    _, planes, x_rows, y_cols = slot_field.shape
    x_length = x_rows * gxs
    sizes = (grps, gxs, gys, x_length, x_length * y_cols * gys * planes)
    fits = (
        grps * gxs * gys == mode_index.shape[0] == 32
        and mix_weight.shape[0] == 64
        and gxs == planes == 2
        and y_cols == 32 * grps == 128
        and x_rows == 48
    )
    if fits:
        return fused(sizes, *arrays)
    return general(*arrays)


def solution(mesh):
    in_specs = (P("grp", None, "gx", "gy"), P(None, "gx", "gy"), P(), P(), P(), P(), P())
    out_specs = (P(None, None, "gx", "gy"), P(("grp", "gx", "gy"), None), P())
    return jax.shard_map(local, mesh=mesh, in_specs=in_specs, out_specs=out_specs, check_vma=False)
```
